768 devices in a mesh: dp: 128 (over y, z_lo, x), tensor: 6 (over z_hi, core).
Axes of the slice: x: 4, y: 8, z: 12 (z_hi: 3, z_lo: 4; z = z_hi * 4 + z_lo), core: 2. Of those that a mesh axis runs over, the one named last changes fastest.
Arguments:
- table_sums: bfloat16 [512, 256, 192], P(None, 'dp', 'tensor'), may hold values from -6 to 6
- bag_lengths: int32 [512, 256], P(None, 'dp'), may hold values from 1 to 8
- feature_slot: int32 [256], replicated, may hold values from 0 to 255, each once
- fm_project: bfloat16 [256, 8], replicated, may hold values from -0.375 to 0.375
- ln_gain: float32 [2048], replicated, may hold values from 0.25 to 1.75
- up_weight: bfloat16 [2048, 6144], P(None, 'tensor'), may hold values from -0.125 to 0.125
- out_weight: bfloat16 [6144, 1536], P('tensor'), may hold values from -0.078125 to 0.078125
- lc_weight: bfloat16 [256, 8], replicated, may hold values from -0.375 to 0.375
- cotangent: bfloat16 [512, 16, 192], P('dp'), may hold values from -6 to 6
Outputs:
- layer_out: bfloat16 [512, 16, 192], P('dp', None, 'tensor')
- grad_sums: bfloat16 [512, 256, 192], P(None, 'dp', 'tensor')
The draws below stay inside these ranges and needn't reach their ends.
Inputs may be any that keep to these rules, and one draw needn't show every extreme that they name: `feature_slot`: each slot number appears once.
All inputs are finite; a program needn't handle non-finite values.
Results may differ from the reference program's by a relative error of at most 0.011.
Values may be sent and summed in bfloat16 or wider, within the bound.
No kernel may reach another device: no remote copies, remote signals or barrier semaphores. Data moves between devices by JAX's collectives and lax.ppermute only.
A program may use at most 64 MiB of HBM per device.

```python
import jax
import jax.numpy as jnp
from jax import lax

F = 256
D = 192
K = 8
NF = 8
NL = 8
H = 6144
SAMPLES = 512


def place_ends(values, rng, low, largest):
    shape = values.shape
    place = [jax.random.randint(jax.random.fold_in(rng, axis), (), 0, shape[axis]) for axis in range(len(shape))]
    values = values.at[tuple(place)].set(low)
    longest = shape.index(max(shape))
    place[longest] = (place[longest] + 1) % shape[longest]
    return values.at[tuple(place)].set(largest)


def block_levels(key, extent, shards, smallest, high):
    loudness = 1.0
    for axis_at, parts in shards:
        heights = jax.random.uniform(jax.random.fold_in(jax.random.fold_in(key, 6), axis_at), (parts,), jnp.float32, smallest / len(shards), high / len(shards))
        loudness = loudness * jnp.repeat(jnp.exp(heights), extent[axis_at] // parts).reshape((-1,) + (1,) * (len(extent) - 1 - axis_at))
    return loudness


def noise(own_key, shape, spread, reach, pieces=(), held_as=jnp.bfloat16):
    loudness = block_levels(own_key, shape, pieces, -0.22, 0.18) if pieces else 1.0
    drawn = jax.random.normal(own_key, shape, jnp.float32) * spread * loudness
    return jnp.minimum(jnp.maximum(drawn, -reach), reach).astype(held_as)


def setup_inputs(seed: int = 0) -> dict:
    key_list = jax.random.split(jax.random.key(seed), 10)
    table_sums = noise(key_list[0], (SAMPLES, F, D), 2.0, 6.0, ((1, 128), (2, 6)))
    bag_lengths = place_ends(jax.random.randint(key_list[1], (SAMPLES, F), 1, 9), jax.random.fold_in(key_list[1], 1), 1, 8).astype(jnp.int32)
    feature_slot = jax.random.permutation(key_list[2], F).astype(jnp.int32)
    fm_project = noise(key_list[3], (F, K), F ** -0.5, 0.375)
    ln_gain = jnp.clip(1.0 + 0.15 * jax.random.normal(key_list[4], (F * K,), jnp.float32), 0.25, 1.75)
    up_weight = noise(key_list[5], (F * K, H), (F * K) ** -0.5, 0.125, ((1, 6),))
    out_weight = noise(key_list[6], (H, NF * D), H ** -0.5, 0.078125, ((0, 6),))
    lc_weight = noise(key_list[7], (F, NL), F ** -0.5, 0.375)
    cotangent = noise(key_list[8], (SAMPLES, NF + NL, D), 1.0, 6.0, ((0, 128),))
    return dict(table_sums=table_sums, bag_lengths=bag_lengths, feature_slot=feature_slot, fm_project=fm_project, ln_gain=ln_gain, up_weight=up_weight, out_weight=out_weight, lc_weight=lc_weight, cotangent=cotangent)


exact_precision = lax.Precision.HIGHEST

def slot_inverse(feature_slot):
    slot_count = feature_slot.shape[0]
    positions = jnp.arange(slot_count, dtype=jnp.int32)
    matches = feature_slot[:, None] == positions[None, :]
    return lax.optimization_barrier(jnp.sum(jnp.where(matches, positions[:, None], 0), axis=0)).astype(jnp.int32)

def reference(table_sums, bag_lengths, feature_slot, fm_project, ln_gain, up_weight, out_weight, lc_weight, cotangent):
    lengths = bag_lengths.astype(jnp.float32)[:, :, None]
    pooled = (table_sums.astype(jnp.float32) / lengths).astype(jnp.bfloat16)
    embedded_features = jnp.take(pooled, feature_slot, axis=1).astype(jnp.float32)
    projection_weight = fm_project.astype(jnp.float32)
    mixing_weight = lc_weight.astype(jnp.float32)
    slot_coupling_matrix = jnp.einsum('sfd,fk->sdk', embedded_features, projection_weight, precision=exact_precision)
    gram_block = jnp.einsum('sfd,sdk->sfk', embedded_features, slot_coupling_matrix, precision=exact_precision)
    flattened = gram_block.reshape(gram_block.shape[0], -1)
    centered = flattened - lax.optimization_barrier(jnp.mean(flattened, axis=1, keepdims=True))
    scale_inv = lax.rsqrt(lax.optimization_barrier(jnp.mean(centered * centered, axis=1, keepdims=True)) + 1e-05)
    whitened = centered * scale_inv
    normed = (whitened * ln_gain).astype(jnp.bfloat16)
    up_proj = jnp.dot(normed, up_weight, preferred_element_type=jnp.float32)
    sigmoid_up = jax.nn.sigmoid(up_proj)
    hidden = (up_proj * sigmoid_up).astype(jnp.bfloat16)
    fm_out = jnp.dot(hidden, out_weight, preferred_element_type=jnp.float32).reshape(SAMPLES, NF, D)
    linear_component = jnp.einsum('gnh,nx->gxh', embedded_features, mixing_weight, precision=exact_precision)
    layer_out = jnp.concatenate([fm_out, linear_component], axis=1).astype(jnp.bfloat16)
    cot_fm = cotangent[:, :NF].reshape(SAMPLES, NF * D)
    d_hidden = jnp.dot(cot_fm, out_weight.T, preferred_element_type=jnp.float32)
    d_up = (d_hidden * (sigmoid_up + up_proj * sigmoid_up * (1.0 - sigmoid_up))).astype(jnp.bfloat16)
    d_norm = jnp.dot(d_up, up_weight.T, preferred_element_type=jnp.float32)
    grad_block = d_norm * ln_gain
    d_flat = scale_inv * (grad_block - lax.optimization_barrier(jnp.mean(grad_block, axis=1, keepdims=True)) - whitened * lax.optimization_barrier(jnp.mean(grad_block * whitened, axis=1, keepdims=True)))
    gram_gradient = d_flat.reshape(gram_block.shape)
    coupling_gradient = jnp.einsum('sfd,sfk->sdk', embedded_features, gram_gradient, precision=exact_precision)
    linear_cotangent_term = cotangent[:, NF:].astype(jnp.float32)
    embedding_gradient = jnp.einsum('tpx,tjx->tpj', gram_gradient, slot_coupling_matrix, precision=exact_precision) + jnp.einsum('zc,jtc->jzt', projection_weight, coupling_gradient, precision=exact_precision) + jnp.einsum('ka,waz->wkz', mixing_weight, linear_cotangent_term, precision=exact_precision)
    d_pooled = jnp.take(embedding_gradient, slot_inverse(feature_slot), axis=1).astype(jnp.bfloat16)
    grad_sums = (d_pooled.astype(jnp.float32) / lengths).astype(jnp.bfloat16)
    return (layer_out, grad_sums)
```

```python
import jax
import jax.numpy as jnp
from jax import lax
from jax.experimental import pallas as pl
from jax.experimental.pallas import tpu as pltpu
from jax.sharding import PartitionSpec as P

F = 256
D = 192
K = 8
NF = 8
S = 4
DW = 32
TP = 6
DP = 128
H = 1024
FK = F * K
ROW = 2 * DW * S
bf16 = jnp.bfloat16
f32 = jnp.float32

VMEM = pl.BlockSpec(memory_space=pltpu.VMEM)


def iota(shape, dim):
    return lax.broadcasted_iota(jnp.int32, shape, dim)


def dot(a, b):
    return jnp.dot(a, b, preferred_element_type=f32)


def dot_nt(a, b):
    return lax.dot_general(a, b, (((1,), (1,)), ((), ())), preferred_element_type=f32)


def split(x):
    hi = x.astype(bf16)
    return hi, (x - hi.astype(f32)).astype(bf16)


def swap_pair(x):
    n = x.shape[1]
    first = (iota(x.shape, 1) // DW) % 2 == 0
    return jnp.where(first, pltpu.roll(x, n - DW, 1), pltpu.roll(x, DW, 1))


def pool_kernel(sums_ref, len_ref, out_ref, scr):
    parts = []
    for j in range(2):
        parts.append(sums_ref[j].astype(f32) / len_ref[j : j + 1, :].astype(f32))
    scr[...] = jnp.concatenate(parts, axis=0).T
    even = scr[pl.ds(0, 256, stride=2), :]
    odd = scr[pl.ds(1, 256, stride=2), :]
    out_ref[...] = jnp.concatenate([even, odd], axis=1).astype(bf16)


def prep_kernel(slot_ref, slot8_ref, fmlc_ref, cot_ref, cotl_ref, ow_ref, vt_ref, v_ref, r_ref, dh_ref, cotb_ref):
    row = iota((F, F), 0)
    place = 2 * (row % DP) + row // DP
    onehot = jnp.where(slot_ref[...] == place, 1.0, 0.0).astype(bf16)
    picked = dot(onehot, fmlc_ref[...])
    a, b = picked[:DP], picked[DP:]
    v_ref[...] = jnp.concatenate(
        [a[:, :K], b[:, :K], a[:, :K], b[:, :K], a[:, K:], b[:, K:]], axis=1
    ).astype(bf16)
    vt_ref[...] = jnp.concatenate([a.T, b.T], axis=0).astype(bf16)
    row8 = iota((F, FK), 0)
    place8 = 2 * (row8 % DP) + row8 // DP
    r_ref[...] = jnp.where(slot8_ref[...] == place8, 1.0, 0.0).astype(bf16)
    dh_ref[...] = dot_nt(cot_ref[...], ow_ref[...])
    c = cotl_ref[...]
    first = (iota(c.shape, 1) // DW) % 2 == 0
    zero = jnp.zeros_like(c)
    cotb_ref[...] = jnp.concatenate([jnp.where(first, c, zero), jnp.where(first, zero, c)], axis=0).astype(bf16)


def own_mask():
    shape = (2 * S * K, ROW)
    r, c = iota(shape, 0), iota(shape, 1)
    return ((r // K) % S == c // (2 * DW)) & (r // (S * K) == (c // DW) % 2)


def gram_kernel(x_ref, vt_ref, g_ref, x_out, cb_ref, lin_ref, scr):
    scr[...] = x_ref[...].astype(f32)
    x = jnp.concatenate(
        [scr[pl.ds(0, DP, stride=2), :], scr[pl.ds(1, DP, stride=2), :]], axis=1
    ).astype(bf16)
    x_out[...] = x
    y = dot(vt_ref[...], x)
    first = (iota((16, ROW), 1) // DW) % 2 == 0
    y = jnp.where(first, y[:16], y[16:])
    y = y + swap_pair(y)
    for s in range(S):
        lin_ref[s] = y[K:, s * 2 * DW : s * 2 * DW + DW].astype(bf16)
    tiled = jnp.concatenate([y[:K]] * (2 * S), axis=0)
    hi, lo = split(jnp.where(own_mask(), tiled, 0.0))
    cb = jnp.concatenate([hi, lo], axis=0)
    cb_ref[...] = cb
    g = dot_nt(cb, x)
    g = (g[:64] + g[64:]).astype(bf16)
    for t in range(TP):
        g_ref[t] = g


def mlp_kernel(g_ref, r_ref, gain_ref, up_ref, ow_ref, dh_ref, c_ref, wh_ref, sc_ref):
    g = g_ref[0].astype(f32)
    for t in range(1, TP):
        g = g + g_ref[t].astype(f32)
    hi, lo = split(jnp.concatenate([g[:32], g[32:]], axis=1))
    m = dot(jnp.concatenate([hi, lo], axis=0), r_ref[...])
    m = m[:32] + m[32:]
    same = iota(m.shape, 0) % K == iota(m.shape, 1) % K
    flat = jnp.sum(jnp.where(same, m, 0.0).reshape(S, K, FK), axis=1)
    centered = flat - jnp.mean(flat, axis=1, keepdims=True)
    scale = lax.rsqrt(jnp.mean(centered * centered, axis=1, keepdims=True) + 1e-05)
    whitened = centered * scale
    wh_ref[...] = whitened
    sc_ref[...] = jnp.broadcast_to(scale, sc_ref.shape)
    normed = (whitened * gain_ref[...]).astype(bf16)
    up = dot(normed, up_ref[...])
    sig = jax.nn.sigmoid(up)
    hidden = (up * sig).astype(bf16)
    d_up = (dh_ref[...] * (sig + up * sig * (1.0 - sig))).astype(bf16)
    fm = dot(hidden, ow_ref[...])
    d_norm = dot_nt(d_up, up_ref[...]).astype(bf16)
    for t in range(TP):
        c_ref[t, :, :FK] = d_norm
        c_ref[t, :, FK:] = jnp.concatenate(
            [fm[:, n * D + t * DW : n * D + (t + 1) * DW] for n in range(NF)], axis=1
        ).astype(bf16)


def grad_kernel(c_ref, r_ref, gain_ref, wh_ref, sc_ref, x_ref, cb_ref, v_ref, cotb_ref, z_ref, fm_ref, scr):
    c = c_ref[0].astype(f32)
    for t in range(1, TP):
        c = c + c_ref[t].astype(f32)
    fm_ref[...] = c[:, FK:]
    wh = wh_ref[...]
    gb = c[:, :FK] * gain_ref[...]
    flat = sc_ref[:, :1] * (
        gb
        - jnp.mean(gb, axis=1, keepdims=True)
        - wh * jnp.mean(gb * wh, axis=1, keepdims=True)
    )
    spread = jnp.broadcast_to(flat[:, None, :], (S, K, FK)).reshape(S * K, FK)
    same = iota(spread.shape, 0) % K == iota(spread.shape, 1) % K
    hi, lo = split(jnp.where(same, spread, 0.0))
    dg = dot_nt(jnp.concatenate([hi, lo], axis=0), r_ref[...])
    dg = dg[:32] + dg[32:]
    dg = jnp.concatenate([dg[:, :DP], dg[:, DP:]], axis=0)
    hi, lo = split(dg)
    x = x_ref[...]
    dc = dot(jnp.concatenate([hi, lo], axis=0), x)
    dc = jnp.where(own_mask(), dc[:64] + dc[64:], 0.0)
    dc = jnp.sum(dc.reshape(2 * S, K, ROW), axis=0)
    dc = dc + swap_pair(dc)
    first = (iota(dc.shape, 1) // DW) % 2 == 0
    zero = jnp.zeros_like(dc)
    dhi, dlo = split(jnp.concatenate([jnp.where(first, dc, zero), jnp.where(first, zero, dc)], axis=0))
    thi, tlo = split(dg.T)
    left = jnp.concatenate([thi, thi, tlo, v_ref[...]], axis=1)
    cb = cb_ref[...]
    right = jnp.concatenate([cb, cb[:64], dhi, dlo, cotb_ref[...]], axis=0)
    z = dot(left, right)
    scr[pl.ds(0, DP, stride=2), :] = z[:, :128]
    scr[pl.ds(1, DP, stride=2), :] = z[:, 128:]
    z_ref[...] = scr[...].astype(bf16)


def unpool_kernel(z_ref, len_ref, out_ref, scr):
    z = z_ref[...].astype(f32)
    scr[pl.ds(0, 256, stride=2), :] = z[:, :64]
    scr[pl.ds(1, 256, stride=2), :] = z[:, 64:]
    zt = scr[...].T
    for j in range(2):
        out_ref[j] = (zt[j * DW : (j + 1) * DW] / len_ref[j : j + 1, :].astype(f32)).astype(bf16)


def call(kernel, outs, args, scratch=(), name=None, cost=None):
    many = len(outs) > 1
    shapes = [jax.ShapeDtypeStruct(s, d) for s, d in outs]
    return pl.pallas_call(
        kernel,
        out_shape=shapes if many else shapes[0],
        in_specs=[VMEM] * len(args),
        out_specs=[VMEM] * len(outs) if many else VMEM,
        scratch_shapes=list(scratch),
        compiler_params=pltpu.CompilerParams(vmem_limit_bytes=8 * 2**20),
        name=name,
        cost_estimate=cost,
    )(*args)


def exchange(x, axis):
    return lax.all_to_all(x, axis, split_axis=0, concat_axis=0, tiled=True)


def shards(
    table_sums,
    bag_lengths,
    feature_slot,
    fm_project,
    ln_gain,
    up_weight,
    out_weight,
    lc_weight,
    cotangent,
):
    sums_t = jnp.transpose(table_sums, (1, 2, 0))
    len_t = jnp.transpose(bag_lengths, (1, 0))
    pooled = call(
        pool_kernel, [((256, 128), bf16)], (sums_t, len_t), [pltpu.VMEM((512, 64), f32)], "pool"
    )
    arrived = exchange(pooled.reshape(DP, 2, 128), "dp").reshape(256, 128)

    slot = feature_slot.reshape(1, F)
    slot8 = jnp.repeat(feature_slot, K).reshape(1, FK)
    fmlc = jnp.concatenate([fm_project, lc_weight], axis=1)
    gain = ln_gain.reshape(1, FK)
    cot_fm = cotangent[:, :NF].reshape(S, NF * D)
    offset = lax.axis_index("tensor") * DW
    cot_l = lax.dynamic_slice_in_dim(cotangent[:, NF:], offset, DW, 2).astype(f32)
    cot_l = jnp.transpose(cot_l, (1, 0, 2))[:, :, None, :]
    cot_l = jnp.broadcast_to(cot_l, (K, S, 2, DW)).reshape(K, ROW)
    vt, v, r, dh, cotb = call(
        prep_kernel,
        [((32, DP), bf16), ((DP, 48), bf16), ((F, FK), bf16), ((S, H), f32), ((16, ROW), bf16)],
        (slot, slot8, fmlc, cot_fm, cot_l, out_weight),
        name="prep",
    )
    g6, x, cb, lin = call(
        gram_kernel,
        [((TP, 64, DP), bf16), ((DP, ROW), bf16), ((128, ROW), bf16), ((S, K, DW), bf16)],
        (arrived, vt),
        [pltpu.VMEM((256, 128), f32)],
        "gram",
    )
    g6 = exchange(g6, "tensor")
    c6, wh, sc = call(
        mlp_kernel,
        [((TP, S, FK + NF * DW), bf16), ((S, FK), f32), ((S, 128), f32)],
        (g6, r, gain, up_weight, out_weight, dh),
        name="mlp",
    )
    c6 = exchange(c6, "tensor")
    z, fm = call(
        grad_kernel,
        [((256, 128), bf16), ((S, NF * DW), f32)],
        (c6, r, gain, wh, sc, x, cb, v, cotb),
        [pltpu.VMEM((256, 128), f32)],
        "grad",
    )
    back = exchange(z.reshape(DP, 2, 128), "dp").reshape(256, 128)
    grad_t = call(
        unpool_kernel, [((2, DW, 512), bf16)], (back, len_t), [pltpu.VMEM((512, 64), f32)], "unpool"
    )
    layer_out = jnp.concatenate([fm.reshape(S, NF, DW).astype(bf16), lin], axis=1)
    return (layer_out, jnp.transpose(grad_t, (2, 0, 1)))


def solution(mesh):
    return jax.shard_map(
        shards,
        mesh=mesh,
        in_specs=(
            P(None, "dp", "tensor"),
            P(None, "dp"),
            P(),
            P(),
            P(),
            P(None, "tensor"),
            P("tensor", None),
            P(),
            P("dp", None, None),
        ),
        out_specs=(P("dp", None, "tensor"), P(None, "dp", "tensor")),
        check_vma=False,
    )
```

```python
import jax
import jax.numpy as jnp
from jax import lax
from jax.experimental import pallas as pl
from jax.experimental.pallas import tpu as pltpu
from jax.sharding import PartitionSpec as P

F = 256
D = 192
K = 8
NF = 8
S = 4
DW = 32
TP = 6
DP = 128
H = 1024
FK = F * K
ROW = DW * S
LARGE = 53_000_000
WHOLE = 66_600_000
CUT = 1024
bf16 = jnp.bfloat16
f32 = jnp.float32

VMEM = pl.BlockSpec(memory_space=pltpu.VMEM)
SMEM = pl.BlockSpec(memory_space=pltpu.SMEM)
HBM = pl.BlockSpec(memory_space=pltpu.HBM)


def iota(shape, dim):
    return lax.broadcasted_iota(jnp.int32, shape, dim)


def dot(a, b):
    return jnp.dot(a, b, preferred_element_type=f32)


def dot_nt(a, b):
    return lax.dot_general(a, b, (((1,), (1,)), ((), ())), preferred_element_type=f32)


def split(x):
    hi = x.astype(bf16)
    return hi, (x - hi.astype(f32)).astype(bf16)


def rows(parts):
    return jnp.concatenate(parts, axis=0)


def lanes(parts):
    return jnp.concatenate(parts, axis=1)


def own_sample():
    shape = (S * K, ROW)
    return iota(shape, 0) // K == iota(shape, 1) // DW


def expander():
    shape = (32, 256)
    return jnp.where(iota(shape, 0) == iota(shape, 1) // K, 1.0, 0.0).astype(bf16)


def own_rank():
    shape = (256, 256)
    return iota(shape, 0) % K == iota(shape, 1) % K


def pool_kernel(sums_hbm, len_hbm, out_ref, sums_ref, len_ref, scr, pairs, sem):
    sums_copy = pltpu.make_async_copy(sums_hbm, sums_ref, sem.at[0])
    len_copy = pltpu.make_async_copy(len_hbm, len_ref, sem.at[1])
    sums_copy.start()
    len_copy.start()
    len_copy.wait()
    length = len_ref[...].astype(f32)
    sums_copy.wait()
    for j in range(2):
        scr[j] = (sums_ref[j].astype(f32) / length[j : j + 1]).T
        pairs[pl.ds(j, DP, stride=2), :] = lanes(
            [scr[j, pl.ds(s, DP, stride=S), :] for s in range(S)]
        )
    out_ref[...] = pairs[...].astype(bf16)


def slot_kernel(slot_ref, fm_ref, lc_ref, hot_ref, vt_ref):
    onehot = jnp.where(slot_ref[...] == iota((F, F), 0), 1.0, 0.0).astype(bf16)
    hot_ref[...] = onehot
    both = rows([fm_ref[...].astype(f32), lc_ref[...].astype(f32)]).astype(bf16)
    vt_ref[...] = dot_nt(both, onehot).astype(bf16)


def gram_kernel(x_ref, vt_ref, hot_ref, g_ref, x_out, cb_ref, lin_ref):
    x = x_ref[...]
    x_out[...] = x
    y = dot(vt_ref[...], x)
    for s in range(S):
        lin_ref[s] = y[K:, s * DW : (s + 1) * DW].astype(bf16)
    hi, lo = split(jnp.where(own_sample(), rows([y[:K]] * S), 0.0))
    cb = rows([hi, lo])
    cb_ref[...] = cb
    g = dot_nt(cb, x)
    g = (g[:32] + g[32:]).astype(bf16)
    g = dot(g, hot_ref[...]).astype(bf16)
    for t in range(TP):
        g_ref[t] = g


def prep_kernel(
    rank_ref, cot_ref, vt_ref, after_ref, up_hbm, ow_hbm, dh_ref, cotl_ref, v_ref, up_out, ow_ref, cot_scr, sem
):
    ow_copy = pltpu.make_async_copy(ow_hbm, ow_ref, sem.at[0])
    up_copy = pltpu.make_async_copy(up_hbm.at[pl.ds(0, CUT)], up_out, sem.at[1])
    ow_copy.start()
    up_copy.start()
    cot_scr[...] = cot_ref[...].astype(f32)
    vt = vt_ref[...].astype(f32)
    v = vt.T
    v_ref[...] = lanes([v[:, :K], v]).astype(bf16)
    rank = rank_ref[0]
    parts = []
    for s in range(S):
        block = cot_scr[s, NF:, :]
        own = jnp.zeros((K, DW), f32)
        for t in range(TP):
            own = jnp.where(rank == t, block[:, t * DW : (t + 1) * DW], own)
        parts.append(own)
    cotl_ref[...] = lanes(parts)
    cot_fm = lanes([cot_scr[:, n, :] for n in range(NF)]).astype(bf16)
    ow_copy.wait()
    dh_ref[...] = dot_nt(cot_fm, ow_ref[...])
    up_copy.wait()


def mlp_kernel(g_ref, gain_ref, dh_ref, lo_ref, up_hbm, ow_hbm, c_ref, wh_ref, sc_ref, hi_ref, ow_ref, sem):
    up_copy = pltpu.make_async_copy(up_hbm.at[pl.ds(CUT, FK - CUT)], hi_ref, sem.at[0])
    ow_copy = pltpu.make_async_copy(ow_hbm, ow_ref, sem.at[1])
    up_copy.start()
    ow_copy.start()
    g = g_ref[0].astype(f32)
    for t in range(1, TP):
        g = g + g_ref[t].astype(f32)
    g = rows([g[:, c * 32 : (c + 1) * 32] for c in range(8)])
    hi, lo = split(g)
    m = dot(rows([hi, lo]), expander())
    m = jnp.where(own_rank(), m[:256] + m[256:], 0.0)
    m = jnp.sum(m.reshape(8 * S, K, 256), axis=1)
    flat = lanes([m[c * S : (c + 1) * S] for c in range(8)])
    centered = flat - jnp.mean(flat, axis=1, keepdims=True)
    scale = lax.rsqrt(jnp.mean(centered * centered, axis=1, keepdims=True) + 1e-05)
    whitened = centered * scale
    wh_ref[...] = whitened
    sc_ref[...] = jnp.broadcast_to(scale, sc_ref.shape)
    normed = (whitened * gain_ref[...]).astype(bf16)
    up = dot(normed[:, :CUT], lo_ref[...])
    up_copy.wait()
    up = up + dot(normed[:, CUT:], hi_ref[...])
    sig = jax.nn.sigmoid(up)
    hidden = (up * sig).astype(bf16)
    d_up = (dh_ref[...] * (sig + up * sig * (1.0 - sig))).astype(bf16)
    d_lo = dot_nt(d_up, lo_ref[...]).astype(bf16)
    d_hi = dot_nt(d_up, hi_ref[...]).astype(bf16)
    ow_copy.wait()
    fm = dot(hidden, ow_ref[...])
    for t in range(TP):
        c_ref[t, :, :CUT] = d_lo
        c_ref[t, :, CUT:FK] = d_hi
        c_ref[t, :, FK:] = lanes(
            [fm[:, n * D + t * DW : n * D + (t + 1) * DW] for n in range(NF)]
        ).astype(bf16)


def grad_kernel(c_ref, gain_ref, wh_ref, sc_ref, x_ref, cb_ref, v_ref, cotl_ref, hot_ref, z_ref, fm_ref):
    c = c_ref[0].astype(f32)
    for t in range(1, TP):
        c = c + c_ref[t].astype(f32)
    fm_ref[...] = c[:, FK:]
    wh = wh_ref[...]
    gb = c[:, :FK] * gain_ref[...]
    flat = sc_ref[:, :1] * (
        gb
        - jnp.mean(gb, axis=1, keepdims=True)
        - wh * jnp.mean(gb * wh, axis=1, keepdims=True)
    )
    spread = rows(
        [
            jnp.broadcast_to(flat[:, None, c * 256 : (c + 1) * 256], (S, K, 256)).reshape(S * K, 256)
            for c in range(8)
        ]
    )
    hi, lo = split(jnp.where(own_rank(), spread, 0.0))
    dg = dot_nt(rows([hi, lo]), expander())
    dg = dg[:256] + dg[256:]
    dg = lanes([dg[c * 32 : (c + 1) * 32] for c in range(8)])
    hi, lo = split(dg)
    dg = dot_nt(rows([hi, lo]), hot_ref[...])
    dc = dot(dg.astype(bf16), x_ref[...])
    dc = jnp.where(own_sample(), dc[:32] + dc[32:], 0.0)
    dc = jnp.sum(dc.reshape(S, K, ROW), axis=0)
    dc_hi = dc.astype(bf16).astype(f32)
    cb = cb_ref[...].astype(f32)
    right = rows([cb[:32], cb[:32], cb[32:], dc_hi, dc - dc_hi, cotl_ref[...]]).astype(bf16)
    dgt = dg.T.astype(bf16)
    left = lanes([dgt, dgt[:, :32], v_ref[...]])
    z_ref[...] = dot(left, right).astype(bf16)


def unpool_kernel(z_ref, len_ref, out_ref, pairs, scr):
    pairs[...] = z_ref[...].astype(f32)
    for j in range(2):
        z = pairs[pl.ds(j, DP, stride=2), :]
        for s in range(S):
            scr[j, pl.ds(s, DP, stride=S), :] = z[:, s * DW : (s + 1) * DW]
        out_ref[j] = (scr[j].T / len_ref[j : j + 1, :].astype(f32)).astype(bf16)


def call(name, kernel, outs, args, specs=None, scratch=(), flops=0, nbytes=0, limit=16 * 2**20):
    many = len(outs) > 1
    shapes = [jax.ShapeDtypeStruct(s, d) for s, d in outs]
    return pl.pallas_call(
        kernel,
        out_shape=shapes if many else shapes[0],
        in_specs=specs or [VMEM] * len(args),
        out_specs=[VMEM] * len(outs) if many else VMEM,
        scratch_shapes=list(scratch),
        compiler_params=pltpu.CompilerParams(vmem_limit_bytes=limit),
        name=name,
        cost_estimate=pl.CostEstimate(flops=flops, bytes_accessed=nbytes, transcendentals=0)
        if flops
        else None,
    )(*args)


def exchange(x, axis):
    return lax.all_to_all(x, axis, split_axis=0, concat_axis=0, tiled=True)


def shards(
    table_sums,
    bag_lengths,
    feature_slot,
    fm_project,
    ln_gain,
    up_weight,
    out_weight,
    lc_weight,
    cotangent,
):
    samples = table_sums.shape[0]
    sums_t = jnp.transpose(table_sums, (1, 2, 0))
    len_t = jnp.transpose(bag_lengths, (1, 0))
    dma = pltpu.SemaphoreType.DMA
    pooled = call(
        "pool",
        pool_kernel,
        [((F, ROW), bf16)],
        (sums_t, len_t),
        [HBM, HBM],
        [
            pltpu.VMEM((2, DW, samples), bf16),
            pltpu.VMEM((2, samples), jnp.int32),
            pltpu.VMEM((2, samples, DW), f32),
            pltpu.VMEM((F, ROW), f32),
            dma((2,)),
        ],
        limit=WHOLE,
    )
    arrived = exchange(pooled.reshape(DP, 2, ROW), "dp").reshape(F, ROW)
    hot, vt = call(
        "slots",
        slot_kernel,
        [((F, F), bf16), ((2 * K, F), bf16)],
        (feature_slot.reshape(1, F), fm_project.T, lc_weight.T),
    )
    g6, x, cb, lin = call(
        "gram",
        gram_kernel,
        [((TP, S * K, F), bf16), ((F, ROW), bf16), ((2 * S * K, ROW), bf16), ((S, K, DW), bf16)],
        (arrived, vt, hot),
    )
    g6 = exchange(g6, "tensor")
    rank = lax.axis_index("tensor").astype(jnp.int32).reshape(1)
    dh, cotl, v, up_lo = call(
        "prep",
        prep_kernel,
        [((S, H), f32), ((K, ROW), f32), ((F, 3 * K), bf16), ((CUT, H), bf16)],
        (rank, cotangent, vt, cb, up_weight, out_weight),
        [SMEM, VMEM, VMEM, VMEM, HBM, HBM],
        [pltpu.VMEM((H, NF * D), bf16), pltpu.VMEM((S, 2 * NF, D), f32), dma((2,))],
        flops=2 * S * H * NF * D,
        nbytes=2 * (H * NF * D + CUT * H),
        limit=LARGE,
    )
    gain = ln_gain.reshape(1, FK)
    c6, wh, sc = call(
        "mlp",
        mlp_kernel,
        [((TP, S, FK + NF * DW), bf16), ((S, FK), f32), ((S, 128), f32)],
        (g6, gain, dh, up_lo, up_weight, out_weight),
        [VMEM, VMEM, VMEM, VMEM, HBM, HBM],
        [pltpu.VMEM((FK - CUT, H), bf16), pltpu.VMEM((H, NF * D), bf16), dma((2,))],
        limit=LARGE,
    )
    c6 = exchange(c6, "tensor")
    z, fm = call(
        "grad",
        grad_kernel,
        [((F, ROW), bf16), ((S, NF * DW), f32)],
        (c6, gain, wh, sc, x, cb, v, cotl, hot),
    )
    back = exchange(z.reshape(DP, 2, ROW), "dp").reshape(F, ROW)
    grad_t = call(
        "unpool",
        unpool_kernel,
        [((2, DW, samples), bf16)],
        (back, len_t),
        None,
        [pltpu.VMEM((F, ROW), f32), pltpu.VMEM((2, samples, DW), f32)],
    )
    layer_out = jnp.concatenate([fm.reshape(S, NF, DW).astype(bf16), lin], axis=1)
    return (layer_out, jnp.transpose(grad_t, (2, 0, 1)))


def solution(mesh):
    return jax.shard_map(
        shards,
        mesh=mesh,
        in_specs=(
            P(None, "dp", "tensor"),
            P(None, "dp"),
            P(),
            P(),
            P(),
            P(None, "tensor"),
            P("tensor", None),
            P(),
            P("dp", None, None),
        ),
        out_specs=(P("dp", None, "tensor"), P(None, "dp", "tensor")),
        check_vma=False,
    )
```

```python
import jax
import jax.numpy as jnp
from jax import lax
from jax.experimental import pallas as pl
from jax.experimental.pallas import tpu as pltpu
from jax.sharding import PartitionSpec as P

F = 256
D = 192
K = 8
NF = 8
S = 4
DW = 32
TP = 6
DP = 128
H = 1024
FK = F * K
ROW = DW * S
LARGE = 53_000_000
WHOLE = 66_600_000
PIECES = 4
CUT = 1024
bf16 = jnp.bfloat16
f32 = jnp.float32

VMEM = pl.BlockSpec(memory_space=pltpu.VMEM)
SMEM = pl.BlockSpec(memory_space=pltpu.SMEM)
HBM = pl.BlockSpec(memory_space=pltpu.HBM)


def iota(shape, dim):
    return lax.broadcasted_iota(jnp.int32, shape, dim)


def dot(a, b):
    return jnp.dot(a, b, preferred_element_type=f32)


def dot_nt(a, b):
    return lax.dot_general(a, b, (((1,), (1,)), ((), ())), preferred_element_type=f32)


def split(x):
    hi = x.astype(bf16)
    return hi, (x - hi.astype(f32)).astype(bf16)


def rows(parts):
    return jnp.concatenate(parts, axis=0)


def lanes(parts):
    return jnp.concatenate(parts, axis=1)


def own_sample():
    shape = (S * K, ROW)
    return iota(shape, 0) // K == iota(shape, 1) // DW


def expander():
    shape = (32, 256)
    return jnp.where(iota(shape, 0) == iota(shape, 1) // K, 1.0, 0.0).astype(bf16)


def own_rank():
    shape = (256, 256)
    return iota(shape, 0) % K == iota(shape, 1) % K


def pool_kernel(sums_hbm, len_hbm, out_ref, sums_ref, len_ref, scr, pairs, sem):
    sums_copy = pltpu.make_async_copy(sums_hbm, sums_ref, sem.at[0])
    len_copy = pltpu.make_async_copy(len_hbm, len_ref, sem.at[1])
    sums_copy.start()
    len_copy.start()
    len_copy.wait()
    length = len_ref[...].astype(f32)
    sums_copy.wait()
    for j in range(2):
        scr[j] = (sums_ref[j].astype(f32) / length[j : j + 1]).T
        pairs[pl.ds(j, DP, stride=2), :] = lanes(
            [scr[j, pl.ds(s, DP, stride=S), :] for s in range(S)]
        )
    out_ref[...] = pairs[...].astype(bf16)


def gram_kernel(x_ref, vt_ref, hot_ref, g_ref, x_out, cb_ref, lin_ref):
    x = x_ref[...]
    x_out[...] = x
    y = dot(vt_ref[...], x)
    for s in range(S):
        lin_ref[s] = y[K:, s * DW : (s + 1) * DW].astype(bf16)
    hi, lo = split(jnp.where(own_sample(), rows([y[:K]] * S), 0.0))
    cb = rows([hi, lo])
    cb_ref[...] = cb
    g = dot_nt(cb, x)
    g = (g[:32] + g[32:]).astype(bf16)
    g = dot(g, hot_ref[...]).astype(bf16)
    for t in range(TP):
        g_ref[t] = g


def prep_kernel(
    rank_ref, slot_ref, fm_ref, lc_ref, cot_ref, up_hbm, ow_hbm,
    hot_ref, vt_ref, dh_ref, cotl_ref, v_ref, up_out, ow_ref, cot_scr, sem,
):
    step = H // PIECES
    ow_copies = [
        pltpu.make_async_copy(ow_hbm.at[pl.ds(p * step, step)], ow_ref.at[pl.ds(p * step, step)], sem.at[p])
        for p in range(PIECES)
    ]
    step_up = CUT // PIECES
    up_copies = [
        pltpu.make_async_copy(
            up_hbm.at[pl.ds(p * step_up, step_up)], up_out.at[pl.ds(p * step_up, step_up)], sem.at[PIECES + p]
        )
        for p in range(PIECES)
    ]
    for copy in ow_copies + up_copies:
        copy.start()
    onehot = jnp.where(slot_ref[...] == iota((F, F), 0), 1.0, 0.0).astype(bf16)
    hot_ref[...] = onehot
    both = rows([fm_ref[...].astype(f32), lc_ref[...].astype(f32)]).astype(bf16)
    vt = dot_nt(both, onehot)
    vt_ref[...] = vt.astype(bf16)
    v = vt.T
    v_ref[...] = lanes([v[:, :K], v]).astype(bf16)
    cot_scr[...] = cot_ref[...].astype(f32)
    rank = rank_ref[0]
    parts = []
    for s in range(S):
        block = cot_scr[s, NF:, :]
        own = jnp.zeros((K, DW), f32)
        for t in range(TP):
            own = jnp.where(rank == t, block[:, t * DW : (t + 1) * DW], own)
        parts.append(own)
    cotl_ref[...] = lanes(parts)
    cot_fm = lanes([cot_scr[:, n, :] for n in range(NF)]).astype(bf16)
    for p in range(PIECES):
        ow_copies[p].wait()
        part = pl.ds(p * step, step)
        dh_ref[:, part] = dot_nt(cot_fm, ow_ref[part, :])
    for copy in up_copies:
        copy.wait()


def mlp_kernel(g_ref, gain_ref, dh_ref, lo_ref, up_hbm, ow_hbm, c_ref, wh_ref, sc_ref, hi_ref, ow_ref, sem):
    step_up = (FK - CUT) // PIECES
    up_copies = [
        pltpu.make_async_copy(
            up_hbm.at[pl.ds(CUT + p * step_up, step_up)], hi_ref.at[pl.ds(p * step_up, step_up)], sem.at[p]
        )
        for p in range(PIECES)
    ]
    step = H // PIECES
    ow_copies = [
        pltpu.make_async_copy(
            ow_hbm.at[pl.ds(p * step, step)], ow_ref.at[pl.ds(p * step, step)], sem.at[PIECES + p]
        )
        for p in range(PIECES)
    ]
    for copy in up_copies + ow_copies:
        copy.start()
    g = g_ref[0].astype(f32)
    for t in range(1, TP):
        g = g + g_ref[t].astype(f32)
    g = rows([g[:, c * 32 : (c + 1) * 32] for c in range(8)])
    hi, lo = split(g)
    m = dot(rows([hi, lo]), expander())
    m = jnp.where(own_rank(), m[:256] + m[256:], 0.0)
    m = jnp.sum(m.reshape(8 * S, K, 256), axis=1)
    flat = lanes([m[c * S : (c + 1) * S] for c in range(8)])
    centered = flat - jnp.mean(flat, axis=1, keepdims=True)
    scale = lax.rsqrt(jnp.mean(centered * centered, axis=1, keepdims=True) + 1e-05)
    whitened = centered * scale
    wh_ref[...] = whitened
    sc_ref[...] = jnp.broadcast_to(scale, sc_ref.shape)
    normed = (whitened * gain_ref[...]).astype(bf16)
    up = dot(normed[:, :CUT], lo_ref[...])
    for copy in up_copies:
        copy.wait()
    up = up + dot(normed[:, CUT:], hi_ref[...])
    sig = jax.nn.sigmoid(up)
    hidden = (up * sig).astype(bf16)
    d_up = (dh_ref[...] * (sig + up * sig * (1.0 - sig))).astype(bf16)
    d_lo = dot_nt(d_up, lo_ref[...]).astype(bf16)
    d_hi = dot_nt(d_up, hi_ref[...]).astype(bf16)
    for copy in ow_copies:
        copy.wait()
    fm = dot(hidden, ow_ref[...])
    for t in range(TP):
        c_ref[t, :, :CUT] = d_lo
        c_ref[t, :, CUT:FK] = d_hi
        c_ref[t, :, FK:] = lanes(
            [fm[:, n * D + t * DW : n * D + (t + 1) * DW] for n in range(NF)]
        ).astype(bf16)


def grad_kernel(c_ref, gain_ref, wh_ref, sc_ref, x_ref, cb_ref, v_ref, cotl_ref, hot_ref, lin_ref, z_ref, layer_hbm, layer_scr, layer_ref, sem):
    c = c_ref[0].astype(f32)
    for t in range(1, TP):
        c = c + c_ref[t].astype(f32)
    for n in range(NF):
        layer_scr[:, n, :] = c[:, FK + n * DW : FK + (n + 1) * DW]
    layer_scr[:, NF:, :] = lin_ref[...].astype(f32)
    layer_ref[...] = layer_scr[...].astype(bf16)
    layer_copy = pltpu.make_async_copy(layer_ref, layer_hbm, sem)
    layer_copy.start()
    wh = wh_ref[...]
    gb = c[:, :FK] * gain_ref[...]
    flat = sc_ref[:, :1] * (
        gb
        - jnp.mean(gb, axis=1, keepdims=True)
        - wh * jnp.mean(gb * wh, axis=1, keepdims=True)
    )
    spread = rows(
        [
            jnp.broadcast_to(flat[:, None, c * 256 : (c + 1) * 256], (S, K, 256)).reshape(S * K, 256)
            for c in range(8)
        ]
    )
    hi, lo = split(jnp.where(own_rank(), spread, 0.0))
    dg = dot_nt(rows([hi, lo]), expander())
    dg = dg[:256] + dg[256:]
    dg = lanes([dg[c * 32 : (c + 1) * 32] for c in range(8)])
    hi, lo = split(dg)
    dg = dot_nt(rows([hi, lo]), hot_ref[...])
    dc = dot(dg.astype(bf16), x_ref[...])
    dc = jnp.where(own_sample(), dc[:32] + dc[32:], 0.0)
    dc = jnp.sum(dc.reshape(S, K, ROW), axis=0)
    dc_hi = dc.astype(bf16).astype(f32)
    cb = cb_ref[...].astype(f32)
    right = rows([cb[:32], cb[:32], cb[32:], dc_hi, dc - dc_hi, cotl_ref[...]]).astype(bf16)
    dgt = dg.T.astype(bf16)
    left = lanes([dgt, dgt[:, :32], v_ref[...]])
    z_ref[...] = dot(left, right).astype(bf16)
    layer_copy.wait()


def unpool_kernel(z_ref, len_ref, out_ref, pairs, scr):
    pairs[...] = z_ref[...].astype(f32)
    for j in range(2):
        z = pairs[pl.ds(j, DP, stride=2), :]
        for s in range(S):
            scr[j, pl.ds(s, DP, stride=S), :] = z[:, s * DW : (s + 1) * DW]
        out_ref[j] = (scr[j].T / len_ref[j : j + 1, :].astype(f32)).astype(bf16)


def call(name, kernel, outs, args, specs=None, scratch=(), flops=0, nbytes=0, limit=16 * 2**20, out_specs=None):
    many = len(outs) > 1
    shapes = [jax.ShapeDtypeStruct(s, d) for s, d in outs]
    return pl.pallas_call(
        kernel,
        out_shape=shapes if many else shapes[0],
        in_specs=specs or [VMEM] * len(args),
        out_specs=out_specs or ([VMEM] * len(outs) if many else VMEM),
        scratch_shapes=list(scratch),
        compiler_params=pltpu.CompilerParams(vmem_limit_bytes=limit),
        name=name,
        cost_estimate=pl.CostEstimate(flops=flops, bytes_accessed=nbytes, transcendentals=0)
        if flops
        else None,
    )(*args)


def exchange(x, axis):
    return lax.all_to_all(x, axis, split_axis=0, concat_axis=0, tiled=True)


def shards(
    table_sums,
    bag_lengths,
    feature_slot,
    fm_project,
    ln_gain,
    up_weight,
    out_weight,
    lc_weight,
    cotangent,
):
    samples = table_sums.shape[0]
    sums_t = jnp.transpose(table_sums, (1, 2, 0))
    len_t = jnp.transpose(bag_lengths, (1, 0))
    dma = pltpu.SemaphoreType.DMA
    pooled = call(
        "pool",
        pool_kernel,
        [((F, ROW), bf16)],
        (sums_t, len_t),
        [HBM, HBM],
        [
            pltpu.VMEM((2, DW, samples), bf16),
            pltpu.VMEM((2, samples), jnp.int32),
            pltpu.VMEM((2, samples, DW), f32),
            pltpu.VMEM((F, ROW), f32),
            dma((2,)),
        ],
        limit=WHOLE,
    )
    arrived = exchange(pooled.reshape(DP, 2, ROW), "dp").reshape(F, ROW)
    rank = lax.axis_index("tensor").astype(jnp.int32).reshape(1)
    hot, vt, dh, cotl, v, up_lo = call(
        "prep",
        prep_kernel,
        [
            ((F, F), bf16),
            ((2 * K, F), bf16),
            ((S, H), f32),
            ((K, ROW), f32),
            ((F, 3 * K), bf16),
            ((CUT, H), bf16),
        ],
        (rank, feature_slot.reshape(1, F), fm_project.T, lc_weight.T, cotangent, up_weight, out_weight),
        [SMEM, VMEM, VMEM, VMEM, VMEM, HBM, HBM],
        [pltpu.VMEM((H, NF * D), bf16), pltpu.VMEM((S, 2 * NF, D), f32), dma((2 * PIECES,))],
        flops=2 * S * H * NF * D,
        nbytes=2 * (H * NF * D + CUT * H),
        limit=LARGE,
    )
    g6, x, cb, lin = call(
        "gram",
        gram_kernel,
        [((TP, S * K, F), bf16), ((F, ROW), bf16), ((2 * S * K, ROW), bf16), ((S, K, DW), bf16)],
        (arrived, vt, hot),
    )
    g6 = exchange(g6, "tensor")
    gain = ln_gain.reshape(1, FK)
    c6, wh, sc = call(
        "mlp",
        mlp_kernel,
        [((TP, S, FK + NF * DW), bf16), ((S, FK), f32), ((S, 128), f32)],
        (g6, gain, dh, up_lo, up_weight, out_weight),
        [VMEM, VMEM, VMEM, VMEM, HBM, HBM],
        [pltpu.VMEM((FK - CUT, H), bf16), pltpu.VMEM((H, NF * D), bf16), dma((2 * PIECES,))],
        limit=LARGE,
    )
    c6 = exchange(c6, "tensor")
    z, layer_out = call(
        "grad",
        grad_kernel,
        [((F, ROW), bf16), ((S, 2 * NF, DW), bf16)],
        (c6, gain, wh, sc, x, cb, v, cotl, hot, lin),
        None,
        [pltpu.VMEM((S, 2 * NF, DW), f32), pltpu.VMEM((S, 2 * NF, DW), bf16), dma],
        out_specs=[VMEM, HBM],
    )
    back = exchange(z.reshape(DP, 2, ROW), "dp").reshape(F, ROW)
    grad_t = call(
        "unpool",
        unpool_kernel,
        [((2, DW, samples), bf16)],
        (back, len_t),
        None,
        [pltpu.VMEM((F, ROW), f32), pltpu.VMEM((2, samples, DW), f32)],
    )
    return (layer_out, jnp.transpose(grad_t, (2, 0, 1)))


def solution(mesh):
    return jax.shard_map(
        shards,
        mesh=mesh,
        in_specs=(
            P(None, "dp", "tensor"),
            P(None, "dp"),
            P(),
            P(),
            P(),
            P(None, "tensor"),
            P("tensor", None),
            P(),
            P("dp", None, None),
        ),
        out_specs=(P("dp", None, "tensor"), P(None, "dp", "tensor")),
        check_vma=False,
    )
```

```python
import jax
import jax.numpy as jnp
from jax import lax
from jax.experimental import pallas as pl
from jax.experimental.pallas import tpu as pltpu
from jax.sharding import PartitionSpec as P

F = 256
D = 192
K = 8
NF = 8
S = 4
DW = 32
TP = 6
TENSOR = ("z_hi", "core")
PEERS = ("core", "z_hi")
DP = 128
H = 1024
FK = F * K
ROW = DW * S
LARGE = 53_000_000
WHOLE = 66_600_000
PIECES = 4
CUT = 1280
bf16 = jnp.bfloat16
f32 = jnp.float32

VMEM = pl.BlockSpec(memory_space=pltpu.VMEM)
SMEM = pl.BlockSpec(memory_space=pltpu.SMEM)
HBM = pl.BlockSpec(memory_space=pltpu.HBM)


def iota(shape, dim):
    return lax.broadcasted_iota(jnp.int32, shape, dim)


def dot(a, b):
    return jnp.dot(a, b, preferred_element_type=f32)


def dot_nt(a, b):
    return lax.dot_general(a, b, (((1,), (1,)), ((), ())), preferred_element_type=f32)


def split(x):
    hi = x.astype(bf16)
    return hi, (x - hi.astype(f32)).astype(bf16)


def rows(parts):
    return jnp.concatenate(parts, axis=0)


def lanes(parts):
    return jnp.concatenate(parts, axis=1)


def own_sample():
    shape = (S * K, ROW)
    return iota(shape, 0) // K == iota(shape, 1) // DW


def expander():
    shape = (32, 256)
    return jnp.where(iota(shape, 0) == iota(shape, 1) // K, 1.0, 0.0).astype(bf16)


def own_rank():
    shape = (256, 256)
    return iota(shape, 0) % K == iota(shape, 1) % K


def pool_kernel(sums_hbm, len_hbm, out_ref, sums_ref, len_ref, scr, pairs, sem):
    sums_copy = pltpu.make_async_copy(sums_hbm, sums_ref, sem.at[0])
    len_copy = pltpu.make_async_copy(len_hbm, len_ref, sem.at[1])
    sums_copy.start()
    len_copy.start()
    len_copy.wait()
    length = len_ref[...].astype(f32)
    sums_copy.wait()
    for j in range(2):
        scr[j] = (sums_ref[j].astype(f32) / length[j : j + 1]).T
        pairs[pl.ds(j, DP, stride=2), :] = lanes(
            [scr[j, pl.ds(s, DP, stride=S), :] for s in range(S)]
        )
    out_ref[...] = pairs[...].astype(bf16)


def gram_kernel(x_ref, vt_ref, hot_ref, g_ref, x_out, cb_ref, lin_ref):
    x = x_ref[...]
    x_out[...] = x
    y = dot(vt_ref[...], x)
    for s in range(S):
        lin_ref[s] = y[K:, s * DW : (s + 1) * DW].astype(bf16)
    hi, lo = split(jnp.where(own_sample(), rows([y[:K]] * S), 0.0))
    cb = rows([hi, lo])
    cb_ref[...] = hi
    g = dot_nt(cb, x)
    g = (g[:32] + g[32:]).reshape(S, K, F)
    mean = jnp.sum(jnp.sum(g, axis=2, keepdims=True), axis=1, keepdims=True) / FK
    g = (g - mean).reshape(S * K, F).astype(bf16)
    g = dot(g, hot_ref[...]).astype(bf16)
    for t in range(TP):
        g_ref[t] = g


def prep_kernel(
    rank_ref, slot_ref, fm_ref, lc_ref, cot_ref, up_hbm, ow_hbm,
    hot_ref, vt_ref, dh_ref, cotl_ref, v_ref, up_out, ow_ref, cot_scr, sem,
):
    step = H // PIECES
    ow_copies = [
        pltpu.make_async_copy(ow_hbm.at[pl.ds(p * step, step)], ow_ref.at[pl.ds(p * step, step)], sem.at[p])
        for p in range(PIECES)
    ]
    step_up = CUT // PIECES
    up_copies = [
        pltpu.make_async_copy(
            up_hbm.at[pl.ds(p * step_up, step_up)], up_out.at[pl.ds(p * step_up, step_up)], sem.at[PIECES + p]
        )
        for p in range(PIECES)
    ]
    for copy in ow_copies + up_copies:
        copy.start()
    onehot = jnp.where(slot_ref[...] == iota((F, F), 0), 1.0, 0.0).astype(bf16)
    hot_ref[...] = onehot
    both = rows([fm_ref[...].astype(f32), lc_ref[...].astype(f32)]).astype(bf16)
    vt = dot_nt(both, onehot)
    vt_ref[...] = vt.astype(bf16)
    v = vt.T
    v_ref[...] = v.astype(bf16)
    cot_scr[...] = cot_ref[...].astype(f32)
    rank = rank_ref[0]
    parts = []
    for s in range(S):
        block = cot_scr[s, NF:, :]
        own = jnp.zeros((K, DW), f32)
        for t in range(TP):
            own = jnp.where(rank == t, block[:, t * DW : (t + 1) * DW], own)
        parts.append(own)
    cotl_ref[...] = lanes(parts)
    cot_fm = lanes([cot_scr[:, n, :] for n in range(NF)]).astype(bf16)
    for p in range(PIECES):
        ow_copies[p].wait()
        part = pl.ds(p * step, step)
        dh_ref[:, part] = dot_nt(cot_fm, ow_ref[part, :])
    for copy in up_copies:
        copy.wait()


def mlp_kernel(g_ref, gain_ref, dh_ref, lo_ref, up_hbm, ow_hbm, c_ref, wh_ref, sc_ref, hi_ref, ow_ref, sem):
    step_up = 256
    up_pieces = (FK - CUT) // step_up
    up_copies = [
        pltpu.make_async_copy(
            up_hbm.at[pl.ds(CUT + p * step_up, step_up)], hi_ref.at[pl.ds(p * step_up, step_up)], sem.at[p]
        )
        for p in range(up_pieces)
    ]
    step = H // PIECES
    ow_copies = [
        pltpu.make_async_copy(
            ow_hbm.at[pl.ds(p * step, step)], ow_ref.at[pl.ds(p * step, step)], sem.at[up_pieces + p]
        )
        for p in range(PIECES)
    ]
    for copy in up_copies + ow_copies:
        copy.start()
    g = g_ref[0].astype(f32)
    for t in range(1, TP):
        g = g + g_ref[t].astype(f32)
    g = rows([g[:, c * 32 : (c + 1) * 32] for c in range(8)])
    m = jnp.where(own_rank(), dot(g.astype(bf16), expander()), 0.0)
    m = jnp.sum(m.reshape(8 * S, K, 256), axis=1)
    flat = lanes([m[c * S : (c + 1) * S] for c in range(8)])
    centered = flat - jnp.mean(flat, axis=1, keepdims=True)
    scale = lax.rsqrt(jnp.mean(centered * centered, axis=1, keepdims=True) + 1e-05)
    whitened = centered * scale
    wh_ref[...] = whitened
    sc_ref[...] = jnp.broadcast_to(scale, sc_ref.shape)
    normed = (whitened * gain_ref[...]).astype(bf16)
    up = dot(normed[:, :CUT], lo_ref[...])
    for p in range(up_pieces):
        up_copies[p].wait()
        part = slice(p * step_up, (p + 1) * step_up)
        up = up + dot(normed[:, CUT + p * step_up : CUT + (p + 1) * step_up], hi_ref[part, :])
    sig = jax.nn.sigmoid(up)
    hidden = (up * sig).astype(bf16)
    d_up = (dh_ref[...] * (sig + up * sig * (1.0 - sig))).astype(bf16)
    d_lo = dot_nt(d_up, lo_ref[...]).astype(bf16)
    d_hi = dot_nt(d_up, hi_ref[...]).astype(bf16)
    fm = jnp.zeros((S, NF * D), f32)
    for p in range(PIECES):
        ow_copies[p].wait()
        fm = fm + dot(hidden[:, p * step : (p + 1) * step], ow_ref[p * step : (p + 1) * step, :])
    for q in range(TP):
        t = (q % 3) * 2 + q // 3
        c_ref[q, :, :CUT] = d_lo
        c_ref[q, :, CUT:FK] = d_hi
        c_ref[q, :, FK:] = lanes(
            [fm[:, n * D + t * DW : n * D + (t + 1) * DW] for n in range(NF)]
        ).astype(bf16)


def grad_kernel(c_ref, gain_ref, wh_ref, sc_ref, x_ref, cb_ref, v_ref, cotl_ref, hot_ref, z_ref, fm_ref):
    c = c_ref[0].astype(f32)
    for t in range(1, TP):
        c = c + c_ref[t].astype(f32)
    fm_ref[...] = c[:, FK:]
    wh = wh_ref[...]
    gb = c[:, :FK] * gain_ref[...]
    flat = sc_ref[:, :1] * (
        gb
        - jnp.mean(gb, axis=1, keepdims=True)
        - wh * jnp.mean(gb * wh, axis=1, keepdims=True)
    )
    spread = rows(
        [
            jnp.broadcast_to(flat[:, None, c * 256 : (c + 1) * 256], (S, K, 256)).reshape(S * K, 256)
            for c in range(8)
        ]
    )
    dg = dot_nt(jnp.where(own_rank(), spread, 0.0).astype(bf16), expander())
    dg = lanes([dg[c * 32 : (c + 1) * 32] for c in range(8)]).astype(bf16)
    dg = dot_nt(dg, hot_ref[...])
    dc = jnp.where(own_sample(), dot(dg.astype(bf16), x_ref[...]), 0.0)
    dc = jnp.sum(dc.reshape(S, K, ROW), axis=0)
    right = rows([cb_ref[...].astype(f32), dc, cotl_ref[...]]).astype(bf16)
    left = lanes([dg.T.astype(bf16), v_ref[...]])
    z_ref[...] = dot(left, right).astype(bf16)


def unpool_kernel(z_ref, len_ref, out_ref, pairs, scr):
    pairs[...] = z_ref[...].astype(f32)
    for j in range(2):
        z = pairs[pl.ds(j, DP, stride=2), :]
        for s in range(S):
            scr[j, pl.ds(s, DP, stride=S), :] = z[:, s * DW : (s + 1) * DW]
        out_ref[j] = (scr[j].T / len_ref[j : j + 1, :].astype(f32)).astype(bf16)


def call(name, kernel, outs, args, specs=None, scratch=(), flops=0, nbytes=0, limit=16 * 2**20):
    many = len(outs) > 1
    shapes = [jax.ShapeDtypeStruct(s, d) for s, d in outs]
    return pl.pallas_call(
        kernel,
        out_shape=shapes if many else shapes[0],
        in_specs=specs or [VMEM] * len(args),
        out_specs=[VMEM] * len(outs) if many else VMEM,
        scratch_shapes=list(scratch),
        compiler_params=pltpu.CompilerParams(vmem_limit_bytes=limit),
        name=name,
        cost_estimate=pl.CostEstimate(flops=flops, bytes_accessed=nbytes, transcendentals=0)
        if flops
        else None,
    )(*args)


def exchange(x, axis):
    return lax.all_to_all(x, axis, split_axis=0, concat_axis=0, tiled=True)


def shards(
    table_sums,
    bag_lengths,
    feature_slot,
    fm_project,
    ln_gain,
    up_weight,
    out_weight,
    lc_weight,
    cotangent,
):
    samples = table_sums.shape[0]
    sums_t = jnp.transpose(table_sums, (1, 2, 0))
    len_t = jnp.transpose(bag_lengths, (1, 0))
    dma = pltpu.SemaphoreType.DMA
    pooled = call(
        "pool",
        pool_kernel,
        [((F, ROW), bf16)],
        (sums_t, len_t),
        [HBM, HBM],
        [
            pltpu.VMEM((2, DW, samples), bf16),
            pltpu.VMEM((2, samples), jnp.int32),
            pltpu.VMEM((2, samples, DW), f32),
            pltpu.VMEM((F, ROW), f32),
            dma((2,)),
        ],
        limit=WHOLE,
    )
    arrived = exchange(pooled.reshape(DP, 2, ROW), "dp").reshape(F, ROW)
    rank = lax.axis_index(TENSOR).astype(jnp.int32).reshape(1)
    hot, vt, dh, cotl, v, up_lo = call(
        "prep",
        prep_kernel,
        [
            ((F, F), bf16),
            ((2 * K, F), bf16),
            ((S, H), f32),
            ((K, ROW), f32),
            ((F, 2 * K), bf16),
            ((CUT, H), bf16),
        ],
        (rank, feature_slot.reshape(1, F), fm_project.T, lc_weight.T, cotangent, up_weight, out_weight),
        [SMEM, VMEM, VMEM, VMEM, VMEM, HBM, HBM],
        [pltpu.VMEM((H, NF * D), bf16), pltpu.VMEM((S, 2 * NF, D), f32), dma((2 * PIECES,))],
        flops=2 * S * H * NF * D,
        nbytes=2 * (H * NF * D + CUT * H),
        limit=LARGE,
    )
    g6, x, cb, lin = call(
        "gram",
        gram_kernel,
        [((TP, S * K, F), bf16), ((F, ROW), bf16), ((S * K, ROW), bf16), ((S, K, DW), bf16)],
        (arrived, vt, hot),
    )
    g6 = exchange(g6, PEERS)
    gain = ln_gain.reshape(1, FK)
    c6, wh, sc = call(
        "mlp",
        mlp_kernel,
        [((TP, S, FK + NF * DW), bf16), ((S, FK), f32), ((S, 128), f32)],
        (g6, gain, dh, up_lo, up_weight, out_weight),
        [VMEM, VMEM, VMEM, VMEM, HBM, HBM],
        [pltpu.VMEM((FK - CUT, H), bf16), pltpu.VMEM((H, NF * D), bf16), dma((2 * PIECES,))],
        limit=LARGE,
    )
    c6 = exchange(c6, PEERS)
    z, fm = call(
        "grad",
        grad_kernel,
        [((F, ROW), bf16), ((S, NF * DW), f32)],
        (c6, gain, wh, sc, x, cb, v, cotl, hot),
    )
    back = exchange(z.reshape(DP, 2, ROW), "dp").reshape(F, ROW)
    grad_t = call(
        "unpool",
        unpool_kernel,
        [((2, DW, samples), bf16)],
        (back, len_t),
        None,
        [pltpu.VMEM((F, ROW), f32), pltpu.VMEM((2, samples, DW), f32)],
    )
    layer_out = jnp.concatenate([fm.reshape(S, NF, DW).astype(bf16), lin], axis=1)
    return (layer_out, jnp.transpose(grad_t, (2, 0, 1)))


def solution(mesh):
    parts = jax.sharding.Mesh(mesh.devices.reshape(DP, 3, 2), ("dp",) + TENSOR)
    return jax.shard_map(
        shards,
        mesh=parts,
        in_specs=(
            P(None, "dp", TENSOR),
            P(None, "dp"),
            P(),
            P(),
            P(),
            P(None, TENSOR),
            P(TENSOR, None),
            P(),
            P("dp", None, None),
        ),
        out_specs=(P("dp", None, TENSOR), P(None, "dp", TENSOR)),
        check_vma=False,
    )
```

```python
import jax
import jax.numpy as jnp
from jax import lax
from jax.experimental import pallas as pl
from jax.experimental.pallas import tpu as pltpu
from jax.sharding import PartitionSpec as P

F = 256
D = 192
K = 8
NF = 8
S = 4
DW = 32
TP = 6
DP = 128
TURN = 79
DP_ORDER = [(q + TURN) % DP for q in range(DP)]
PEERS = [4, 0, 2, 5, 1, 3]
H = 1024
FK = F * K
ROW = DW * S
LARGE = 53_000_000
WHOLE = 66_600_000
CUT = 1024
bf16 = jnp.bfloat16
f32 = jnp.float32

VMEM = pl.BlockSpec(memory_space=pltpu.VMEM)
SMEM = pl.BlockSpec(memory_space=pltpu.SMEM)
HBM = pl.BlockSpec(memory_space=pltpu.HBM)


def iota(shape, dim):
    return lax.broadcasted_iota(jnp.int32, shape, dim)


def dot(a, b):
    return jnp.dot(a, b, preferred_element_type=f32)


def dot_nt(a, b):
    return lax.dot_general(a, b, (((1,), (1,)), ((), ())), preferred_element_type=f32)


def split(x):
    hi = x.astype(bf16)
    return hi, (x - hi.astype(f32)).astype(bf16)


def rows(parts):
    return jnp.concatenate(parts, axis=0)


def lanes(parts):
    return jnp.concatenate(parts, axis=1)


def own_sample():
    shape = (S * K, ROW)
    return iota(shape, 0) // K == iota(shape, 1) // DW


def expander():
    shape = (32, 256)
    return jnp.where(iota(shape, 0) == iota(shape, 1) // K, 1.0, 0.0).astype(bf16)


def own_rank():
    shape = (256, 256)
    return iota(shape, 0) % K == iota(shape, 1) % K


def pool_kernel(sums_hbm, len_hbm, out_ref, sums_ref, len_ref, scr, pairs, sem):
    sums_copy = pltpu.make_async_copy(sums_hbm, sums_ref, sem.at[0])
    len_copy = pltpu.make_async_copy(len_hbm, len_ref, sem.at[1])
    sums_copy.start()
    len_copy.start()
    len_copy.wait()
    length = len_ref[...].astype(f32)
    sums_copy.wait()
    for j in range(2):
        scr[j] = (sums_ref[j].astype(f32) / length[j : j + 1]).T
        pairs[pl.ds(j, DP, stride=2), :] = lanes(
            [scr[j, pl.ds(s, DP, stride=S), :] for s in range(S)]
        )
    turned = rows([pairs[2 * TURN :, :], pairs[: 2 * TURN, :]]) if TURN else pairs[...]
    out_ref[...] = turned.astype(bf16)


def slot_kernel(slot_ref, fm_ref, lc_ref, hot_ref, vt_ref):
    onehot = jnp.where(slot_ref[...] == (iota((F, F), 0) + 2 * TURN) % F, 1.0, 0.0).astype(bf16)
    hot_ref[...] = onehot
    both = rows([fm_ref[...].astype(f32), lc_ref[...].astype(f32)]).astype(bf16)
    vt_ref[...] = dot_nt(both, onehot).astype(bf16)


def gram_kernel(x_ref, vt_ref, hot_ref, g_ref, x_out, cb_ref, lin_ref):
    x = x_ref[...]
    x_out[...] = x
    y = dot(vt_ref[...], x)
    for s in range(S):
        lin_ref[s] = y[K:, s * DW : (s + 1) * DW].astype(bf16)
    hi, lo = split(jnp.where(own_sample(), rows([y[:K]] * S), 0.0))
    cb = rows([hi, lo])
    cb_ref[...] = cb
    g = dot_nt(cb, x)
    g = (g[:32] + g[32:]).astype(bf16)
    g = dot(g, hot_ref[...]).astype(bf16)
    for t in range(TP):
        g_ref[t] = g


def prep_kernel(
    rank_ref, cot_ref, vt_ref, after_ref, up_hbm, ow_hbm, dh_ref, cotl_ref, v_ref, up_out, ow_ref, cot_scr, sem
):
    ow_copy = pltpu.make_async_copy(ow_hbm, ow_ref, sem.at[0])
    up_copy = pltpu.make_async_copy(up_hbm.at[pl.ds(0, CUT)], up_out, sem.at[1])
    ow_copy.start()
    up_copy.start()
    cot_scr[...] = cot_ref[...].astype(f32)
    vt = vt_ref[...].astype(f32)
    v = vt.T
    v_ref[...] = lanes([v[:, :K], v]).astype(bf16)
    rank = rank_ref[0]
    parts = []
    for s in range(S):
        block = cot_scr[s, NF:, :]
        own = jnp.zeros((K, DW), f32)
        for t in range(TP):
            own = jnp.where(rank == t, block[:, t * DW : (t + 1) * DW], own)
        parts.append(own)
    cotl_ref[...] = lanes(parts)
    cot_fm = lanes([cot_scr[:, n, :] for n in range(NF)]).astype(bf16)
    ow_copy.wait()
    dh_ref[...] = dot_nt(cot_fm, ow_ref[...])
    up_copy.wait()


def mlp_kernel(g_ref, gain_ref, dh_ref, lo_ref, up_hbm, ow_hbm, c_ref, wh_ref, sc_ref, hi_ref, ow_ref, sem):
    up_copy = pltpu.make_async_copy(up_hbm.at[pl.ds(CUT, FK - CUT)], hi_ref, sem.at[0])
    ow_copy = pltpu.make_async_copy(ow_hbm, ow_ref, sem.at[1])
    up_copy.start()
    ow_copy.start()
    g = g_ref[0].astype(f32)
    for t in range(1, TP):
        g = g + g_ref[t].astype(f32)
    g = rows([g[:, c * 32 : (c + 1) * 32] for c in range(8)])
    hi, lo = split(g)
    m = dot(rows([hi, lo]), expander())
    m = jnp.where(own_rank(), m[:256] + m[256:], 0.0)
    m = jnp.sum(m.reshape(8 * S, K, 256), axis=1)
    flat = lanes([m[c * S : (c + 1) * S] for c in range(8)])
    centered = flat - jnp.mean(flat, axis=1, keepdims=True)
    scale = lax.rsqrt(jnp.mean(centered * centered, axis=1, keepdims=True) + 1e-05)
    whitened = centered * scale
    wh_ref[...] = whitened
    sc_ref[...] = jnp.broadcast_to(scale, sc_ref.shape)
    normed = (whitened * gain_ref[...]).astype(bf16)
    up = dot(normed[:, :CUT], lo_ref[...])
    up_copy.wait()
    up = up + dot(normed[:, CUT:], hi_ref[...])
    sig = jax.nn.sigmoid(up)
    hidden = (up * sig).astype(bf16)
    d_up = (dh_ref[...] * (sig + up * sig * (1.0 - sig))).astype(bf16)
    d_lo = dot_nt(d_up, lo_ref[...]).astype(bf16)
    d_hi = dot_nt(d_up, hi_ref[...]).astype(bf16)
    ow_copy.wait()
    fm = dot(hidden, ow_ref[...])
    for q in range(TP):
        t = PEERS[q]
        c_ref[q, :, :CUT] = d_lo
        c_ref[q, :, CUT:FK] = d_hi
        c_ref[q, :, FK:] = lanes(
            [fm[:, n * D + t * DW : n * D + (t + 1) * DW] for n in range(NF)]
        ).astype(bf16)


def grad_kernel(c_ref, gain_ref, wh_ref, sc_ref, x_ref, cb_ref, v_ref, cotl_ref, hot_ref, z_ref, fm_ref):
    c = c_ref[0].astype(f32)
    for t in range(1, TP):
        c = c + c_ref[t].astype(f32)
    fm_ref[...] = c[:, FK:]
    wh = wh_ref[...]
    gb = c[:, :FK] * gain_ref[...]
    flat = sc_ref[:, :1] * (
        gb
        - jnp.mean(gb, axis=1, keepdims=True)
        - wh * jnp.mean(gb * wh, axis=1, keepdims=True)
    )
    spread = rows(
        [
            jnp.broadcast_to(flat[:, None, c * 256 : (c + 1) * 256], (S, K, 256)).reshape(S * K, 256)
            for c in range(8)
        ]
    )
    hi, lo = split(jnp.where(own_rank(), spread, 0.0))
    dg = dot_nt(rows([hi, lo]), expander())
    dg = dg[:256] + dg[256:]
    dg = lanes([dg[c * 32 : (c + 1) * 32] for c in range(8)])
    hi, lo = split(dg)
    dg = dot_nt(rows([hi, lo]), hot_ref[...])
    dc = dot(dg.astype(bf16), x_ref[...])
    dc = jnp.where(own_sample(), dc[:32] + dc[32:], 0.0)
    dc = jnp.sum(dc.reshape(S, K, ROW), axis=0)
    dc_hi = dc.astype(bf16).astype(f32)
    cb = cb_ref[...].astype(f32)
    right = rows([cb[:32], cb[:32], cb[32:], dc_hi, dc - dc_hi, cotl_ref[...]]).astype(bf16)
    dgt = dg.T.astype(bf16)
    left = lanes([dgt, dgt[:, :32], v_ref[...]])
    z_ref[...] = dot(left, right).astype(bf16)


def unpool_kernel(z_ref, len_ref, out_ref, pairs, scr):
    z = z_ref[...].astype(f32)
    pairs[...] = rows([z[F - 2 * TURN :], z[: F - 2 * TURN]]) if TURN else z
    for j in range(2):
        z = pairs[pl.ds(j, DP, stride=2), :]
        for s in range(S):
            scr[j, pl.ds(s, DP, stride=S), :] = z[:, s * DW : (s + 1) * DW]
        out_ref[j] = (scr[j].T / len_ref[j : j + 1, :].astype(f32)).astype(bf16)


def call(name, kernel, outs, args, specs=None, scratch=(), flops=0, nbytes=0, limit=16 * 2**20):
    many = len(outs) > 1
    shapes = [jax.ShapeDtypeStruct(s, d) for s, d in outs]
    return pl.pallas_call(
        kernel,
        out_shape=shapes if many else shapes[0],
        in_specs=specs or [VMEM] * len(args),
        out_specs=[VMEM] * len(outs) if many else VMEM,
        scratch_shapes=list(scratch),
        compiler_params=pltpu.CompilerParams(vmem_limit_bytes=limit),
        name=name,
        cost_estimate=pl.CostEstimate(flops=flops, bytes_accessed=nbytes, transcendentals=0)
        if flops
        else None,
    )(*args)


def exchange(x, axis, order):
    return lax.all_to_all(x, axis, split_axis=0, concat_axis=0, axis_index_groups=[order], tiled=True)


def shards(
    table_sums,
    bag_lengths,
    feature_slot,
    fm_project,
    ln_gain,
    up_weight,
    out_weight,
    lc_weight,
    cotangent,
):
    samples = table_sums.shape[0]
    sums_t = jnp.transpose(table_sums, (1, 2, 0))
    len_t = jnp.transpose(bag_lengths, (1, 0))
    dma = pltpu.SemaphoreType.DMA
    pooled = call(
        "pool",
        pool_kernel,
        [((F, ROW), bf16)],
        (sums_t, len_t),
        [HBM, HBM],
        [
            pltpu.VMEM((2, DW, samples), bf16),
            pltpu.VMEM((2, samples), jnp.int32),
            pltpu.VMEM((2, samples, DW), f32),
            pltpu.VMEM((F, ROW), f32),
            dma((2,)),
        ],
        limit=WHOLE,
    )
    arrived = exchange(pooled.reshape(DP, 2, ROW), "dp", DP_ORDER).reshape(F, ROW)
    hot, vt = call(
        "slots",
        slot_kernel,
        [((F, F), bf16), ((2 * K, F), bf16)],
        (feature_slot.reshape(1, F), fm_project.T, lc_weight.T),
    )
    g6, x, cb, lin = call(
        "gram",
        gram_kernel,
        [((TP, S * K, F), bf16), ((F, ROW), bf16), ((2 * S * K, ROW), bf16), ((S, K, DW), bf16)],
        (arrived, vt, hot),
    )
    g6 = exchange(g6, "tensor", PEERS)
    rank = lax.axis_index("tensor").astype(jnp.int32).reshape(1)
    dh, cotl, v, up_lo = call(
        "prep",
        prep_kernel,
        [((S, H), f32), ((K, ROW), f32), ((F, 3 * K), bf16), ((CUT, H), bf16)],
        (rank, cotangent, vt, cb, up_weight, out_weight),
        [SMEM, VMEM, VMEM, VMEM, HBM, HBM],
        [pltpu.VMEM((H, NF * D), bf16), pltpu.VMEM((S, 2 * NF, D), f32), dma((2,))],
        flops=2 * S * H * NF * D,
        nbytes=2 * (H * NF * D + CUT * H),
        limit=LARGE,
    )
    gain = ln_gain.reshape(1, FK)
    c6, wh, sc = call(
        "mlp",
        mlp_kernel,
        [((TP, S, FK + NF * DW), bf16), ((S, FK), f32), ((S, 128), f32)],
        (g6, gain, dh, up_lo, up_weight, out_weight),
        [VMEM, VMEM, VMEM, VMEM, HBM, HBM],
        [pltpu.VMEM((FK - CUT, H), bf16), pltpu.VMEM((H, NF * D), bf16), dma((2,))],
        limit=LARGE,
    )
    c6 = exchange(c6, "tensor", PEERS)
    z, fm = call(
        "grad",
        grad_kernel,
        [((F, ROW), bf16), ((S, NF * DW), f32)],
        (c6, gain, wh, sc, x, cb, v, cotl, hot),
    )
    back = exchange(z.reshape(DP, 2, ROW), "dp", DP_ORDER).reshape(F, ROW)
    grad_t = call(
        "unpool",
        unpool_kernel,
        [((2, DW, samples), bf16)],
        (back, len_t),
        None,
        [pltpu.VMEM((F, ROW), f32), pltpu.VMEM((2, samples, DW), f32)],
    )
    layer_out = jnp.concatenate([fm.reshape(S, NF, DW).astype(bf16), lin], axis=1)
    return (layer_out, jnp.transpose(grad_t, (2, 0, 1)))


def solution(mesh):
    return jax.shard_map(
        shards,
        mesh=mesh,
        in_specs=(
            P(None, "dp", "tensor"),
            P(None, "dp"),
            P(),
            P(),
            P(),
            P(None, "tensor"),
            P("tensor", None),
            P(),
            P("dp", None, None),
        ),
        out_specs=(P("dp", None, "tensor"), P(None, "dp", "tensor")),
        check_vma=False,
    )
```

```python
import jax
import jax.numpy as jnp
from jax import lax
from jax.experimental import pallas as pl
from jax.experimental.pallas import tpu as pltpu
from jax.sharding import PartitionSpec as P

F = 256
D = 192
K = 8
NF = 8
S = 4
DW = 32
TP = 6
DP = 128
TURN = 79
DP_ORDER = [(q + TURN) % DP for q in range(DP)]
PEERS = [4, 0, 2, 5, 1, 3]
H = 1024
FK = F * K
ROW = DW * S
LARGE = 53_000_000
WHOLE = 66_600_000
CUT = 1024
bf16 = jnp.bfloat16
f32 = jnp.float32

VMEM = pl.BlockSpec(memory_space=pltpu.VMEM)
SMEM = pl.BlockSpec(memory_space=pltpu.SMEM)
HBM = pl.BlockSpec(memory_space=pltpu.HBM)


def iota(shape, dim):
    return lax.broadcasted_iota(jnp.int32, shape, dim)


def dot(a, b):
    return jnp.dot(a, b, preferred_element_type=f32)


def dot_nt(a, b):
    return lax.dot_general(a, b, (((1,), (1,)), ((), ())), preferred_element_type=f32)


def split(x):
    hi = x.astype(bf16)
    return hi, (x - hi.astype(f32)).astype(bf16)


def rows(parts):
    return jnp.concatenate(parts, axis=0)


def lanes(parts):
    return jnp.concatenate(parts, axis=1)


def own_sample():
    shape = (S * K, ROW)
    return iota(shape, 0) // K == iota(shape, 1) // DW


def expander():
    shape = (32, 256)
    return jnp.where(iota(shape, 0) == iota(shape, 1) // K, 1.0, 0.0).astype(bf16)


def own_rank():
    shape = (256, 256)
    return iota(shape, 0) % K == iota(shape, 1) % K


def pool_kernel(sums_hbm, len_hbm, out_ref, sums_ref, len_ref, scr, pairs, sem):
    sums_copy = pltpu.make_async_copy(sums_hbm, sums_ref, sem.at[0])
    len_copy = pltpu.make_async_copy(len_hbm, len_ref, sem.at[1])
    sums_copy.start()
    len_copy.start()
    len_copy.wait()
    length = len_ref[...].astype(f32)
    sums_copy.wait()
    for j in range(2):
        scr[j] = (sums_ref[j].astype(f32) / length[j : j + 1]).T
        pairs[pl.ds(j, DP, stride=2), :] = lanes(
            [scr[j, pl.ds(s, DP, stride=S), :] for s in range(S)]
        )
    turned = rows([pairs[2 * TURN :, :], pairs[: 2 * TURN, :]]) if TURN else pairs[...]
    out_ref[...] = turned.astype(bf16)


def slot_kernel(slot_ref, fm_ref, lc_ref, hot_ref, vt_ref):
    onehot = jnp.where(slot_ref[...] == (iota((F, F), 0) + 2 * TURN) % F, 1.0, 0.0).astype(bf16)
    hot_ref[...] = onehot
    both = rows([fm_ref[...].astype(f32), lc_ref[...].astype(f32)]).astype(bf16)
    vt_ref[...] = dot_nt(both, onehot).astype(bf16)


def gram_kernel(x_ref, vt_ref, hot_ref, g_ref, x_out, cb_ref, lin_ref):
    x = x_ref[...]
    x_out[...] = x
    y = dot(vt_ref[...], x)
    for s in range(S):
        lin_ref[s] = y[K:, s * DW : (s + 1) * DW].astype(bf16)
    hi, lo = split(jnp.where(own_sample(), rows([y[:K]] * S), 0.0))
    cb = rows([hi, lo])
    cb_ref[...] = cb
    g = dot_nt(cb, x)
    g = (g[:32] + g[32:]).astype(bf16)
    g = dot(g, hot_ref[...]).astype(bf16)
    for t in range(TP):
        g_ref[t] = g


def prep_kernel(
    rank_ref, cot_ref, vt_ref, after_ref, up_hbm, ow_hbm, dh_ref, cotl_ref, v_ref, up_out, ow_ref, cot_scr, sem
):
    ow_copy = pltpu.make_async_copy(ow_hbm, ow_ref, sem.at[0])
    up_copy = pltpu.make_async_copy(up_hbm.at[pl.ds(0, CUT)], up_out, sem.at[1])
    ow_copy.start()
    up_copy.start()
    cot_scr[...] = cot_ref[...].astype(f32)
    vt = vt_ref[...].astype(f32)
    v = vt.T
    v_ref[...] = lanes([v[:, :K], v]).astype(bf16)
    rank = rank_ref[0]
    parts = []
    for s in range(S):
        block = cot_scr[s, NF:, :]
        own = jnp.zeros((K, DW), f32)
        for t in range(TP):
            own = jnp.where(rank == t, block[:, t * DW : (t + 1) * DW], own)
        parts.append(own)
    cotl_ref[...] = lanes(parts)
    cot_fm = lanes([cot_scr[:, n, :] for n in range(NF)]).astype(bf16)
    ow_copy.wait()
    dh_ref[...] = dot_nt(cot_fm, ow_ref[...])
    up_copy.wait()


def mlp_kernel(g_ref, gain_ref, dh_ref, lo_ref, up_hbm, ow_hbm, c_ref, wh_ref, sc_ref, hi_ref, ow_ref, sem):
    up_copy = pltpu.make_async_copy(up_hbm.at[pl.ds(CUT, FK - CUT)], hi_ref, sem.at[0])
    ow_copy = pltpu.make_async_copy(ow_hbm, ow_ref, sem.at[1])
    up_copy.start()
    ow_copy.start()
    g = g_ref[0].astype(f32)
    for t in range(1, TP):
        g = g + g_ref[t].astype(f32)
    g = rows([g[:, c * 32 : (c + 1) * 32] for c in range(8)])
    hi, lo = split(g)
    m = dot(rows([hi, lo]), expander())
    m = jnp.where(own_rank(), m[:256] + m[256:], 0.0)
    m = jnp.sum(m.reshape(8 * S, K, 256), axis=1)
    flat = lanes([m[c * S : (c + 1) * S] for c in range(8)])
    centered = flat - jnp.mean(flat, axis=1, keepdims=True)
    scale = lax.rsqrt(jnp.mean(centered * centered, axis=1, keepdims=True) + 1e-05)
    whitened = centered * scale
    wh_ref[...] = whitened
    sc_ref[...] = jnp.broadcast_to(scale, sc_ref.shape)
    normed = (whitened * gain_ref[...]).astype(bf16)
    up = dot(normed[:, :CUT], lo_ref[...])
    up_copy.wait()
    up = up + dot(normed[:, CUT:], hi_ref[...])
    sig = jax.nn.sigmoid(up)
    hidden = (up * sig).astype(bf16)
    d_up = (dh_ref[...] * (sig + up * sig * (1.0 - sig))).astype(bf16)
    d_lo = dot_nt(d_up, lo_ref[...]).astype(bf16)
    d_hi = dot_nt(d_up, hi_ref[...]).astype(bf16)
    ow_copy.wait()
    fm = dot(hidden, ow_ref[...])
    for q in range(TP):
        t = PEERS[q]
        c_ref[q, :, :CUT] = d_lo
        c_ref[q, :, CUT:FK] = d_hi
        c_ref[q, :, FK:] = lanes(
            [fm[:, n * D + t * DW : n * D + (t + 1) * DW] for n in range(NF)]
        ).astype(bf16)


def grad_kernel(c_ref, gain_ref, wh_ref, sc_ref, x_ref, cb_ref, v_ref, cotl_ref, hot_ref, z_ref, fm_ref):
    c = c_ref[0].astype(f32)
    for t in range(1, TP):
        c = c + c_ref[t].astype(f32)
    fm_ref[...] = c[:, FK:]
    wh = wh_ref[...]
    gb = c[:, :FK] * gain_ref[...]
    flat = sc_ref[:, :1] * (
        gb
        - jnp.mean(gb, axis=1, keepdims=True)
        - wh * jnp.mean(gb * wh, axis=1, keepdims=True)
    )
    spread = rows(
        [
            jnp.broadcast_to(flat[:, None, c * 256 : (c + 1) * 256], (S, K, 256)).reshape(S * K, 256)
            for c in range(8)
        ]
    )
    hi, lo = split(jnp.where(own_rank(), spread, 0.0))
    dg = dot_nt(rows([hi, lo]), expander())
    dg = dg[:256] + dg[256:]
    dg = lanes([dg[c * 32 : (c + 1) * 32] for c in range(8)])
    hi, lo = split(dg)
    dg = dot_nt(rows([hi, lo]), hot_ref[...])
    dc = dot(dg.astype(bf16), x_ref[...])
    dc = jnp.where(own_sample(), dc[:32] + dc[32:], 0.0)
    dc = jnp.sum(dc.reshape(S, K, ROW), axis=0)
    dc_hi = dc.astype(bf16).astype(f32)
    cb = cb_ref[...].astype(f32)
    right = rows([cb[:32], cb[:32], cb[32:], dc_hi, dc - dc_hi, cotl_ref[...]]).astype(bf16)
    dgt = dg.T.astype(bf16)
    left = lanes([dgt, dgt[:, :32], v_ref[...]])
    z_ref[...] = dot(left, right).astype(bf16)


def unpool_kernel(z_ref, len_ref, fm_ref, lin_ref, out_ref, layer_ref, pairs, scr, layer):
    for n in range(NF):
        layer[:, n, :] = fm_ref[:, n * DW : (n + 1) * DW]
    layer[:, NF:, :] = lin_ref[...].astype(f32)
    layer_ref[...] = layer[...].astype(bf16)
    z = z_ref[...].astype(f32)
    pairs[...] = rows([z[F - 2 * TURN :], z[: F - 2 * TURN]]) if TURN else z
    for j in range(2):
        z = pairs[pl.ds(j, DP, stride=2), :]
        for s in range(S):
            scr[j, pl.ds(s, DP, stride=S), :] = z[:, s * DW : (s + 1) * DW]
        out_ref[j] = (scr[j].T / len_ref[j : j + 1, :].astype(f32)).astype(bf16)


def call(name, kernel, outs, args, specs=None, scratch=(), flops=0, nbytes=0, limit=16 * 2**20):
    many = len(outs) > 1
    shapes = [jax.ShapeDtypeStruct(s, d) for s, d in outs]
    return pl.pallas_call(
        kernel,
        out_shape=shapes if many else shapes[0],
        in_specs=specs or [VMEM] * len(args),
        out_specs=[VMEM] * len(outs) if many else VMEM,
        scratch_shapes=list(scratch),
        compiler_params=pltpu.CompilerParams(vmem_limit_bytes=limit),
        name=name,
        cost_estimate=pl.CostEstimate(flops=flops, bytes_accessed=nbytes, transcendentals=0)
        if flops
        else None,
    )(*args)


def exchange(x, axis, order):
    return lax.all_to_all(x, axis, split_axis=0, concat_axis=0, axis_index_groups=[order], tiled=True)


def shards(
    table_sums,
    bag_lengths,
    feature_slot,
    fm_project,
    ln_gain,
    up_weight,
    out_weight,
    lc_weight,
    cotangent,
):
    samples = table_sums.shape[0]
    sums_t = jnp.transpose(table_sums, (1, 2, 0))
    len_t = jnp.transpose(bag_lengths, (1, 0))
    dma = pltpu.SemaphoreType.DMA
    pooled = call(
        "pool",
        pool_kernel,
        [((F, ROW), bf16)],
        (sums_t, len_t),
        [HBM, HBM],
        [
            pltpu.VMEM((2, DW, samples), bf16),
            pltpu.VMEM((2, samples), jnp.int32),
            pltpu.VMEM((2, samples, DW), f32),
            pltpu.VMEM((F, ROW), f32),
            dma((2,)),
        ],
        limit=WHOLE,
    )
    arrived = exchange(pooled.reshape(DP, 2, ROW), "dp", DP_ORDER).reshape(F, ROW)
    hot, vt = call(
        "slots",
        slot_kernel,
        [((F, F), bf16), ((2 * K, F), bf16)],
        (feature_slot.reshape(1, F), fm_project.T, lc_weight.T),
    )
    g6, x, cb, lin = call(
        "gram",
        gram_kernel,
        [((TP, S * K, F), bf16), ((F, ROW), bf16), ((2 * S * K, ROW), bf16), ((S, K, DW), bf16)],
        (arrived, vt, hot),
    )
    g6 = exchange(g6, "tensor", PEERS)
    rank = lax.axis_index("tensor").astype(jnp.int32).reshape(1)
    dh, cotl, v, up_lo = call(
        "prep",
        prep_kernel,
        [((S, H), f32), ((K, ROW), f32), ((F, 3 * K), bf16), ((CUT, H), bf16)],
        (rank, cotangent, vt, cb, up_weight, out_weight),
        [SMEM, VMEM, VMEM, VMEM, HBM, HBM],
        [pltpu.VMEM((H, NF * D), bf16), pltpu.VMEM((S, 2 * NF, D), f32), dma((2,))],
        flops=2 * S * H * NF * D,
        nbytes=2 * (H * NF * D + CUT * H),
        limit=LARGE,
    )
    gain = ln_gain.reshape(1, FK)
    c6, wh, sc = call(
        "mlp",
        mlp_kernel,
        [((TP, S, FK + NF * DW), bf16), ((S, FK), f32), ((S, 128), f32)],
        (g6, gain, dh, up_lo, up_weight, out_weight),
        [VMEM, VMEM, VMEM, VMEM, HBM, HBM],
        [pltpu.VMEM((FK - CUT, H), bf16), pltpu.VMEM((H, NF * D), bf16), dma((2,))],
        limit=LARGE,
    )
    c6 = exchange(c6, "tensor", PEERS)
    z, fm = call(
        "grad",
        grad_kernel,
        [((F, ROW), bf16), ((S, NF * DW), f32)],
        (c6, gain, wh, sc, x, cb, v, cotl, hot),
    )
    back = exchange(z.reshape(DP, 2, ROW), "dp", DP_ORDER).reshape(F, ROW)
    grad_t, layer_out = call(
        "unpool",
        unpool_kernel,
        [((2, DW, samples), bf16), ((S, 2 * NF, DW), bf16)],
        (back, len_t, fm, lin),
        None,
        [pltpu.VMEM((F, ROW), f32), pltpu.VMEM((2, samples, DW), f32), pltpu.VMEM((S, 2 * NF, DW), f32)],
    )
    return (layer_out, jnp.transpose(grad_t, (2, 0, 1)))


def solution(mesh):
    return jax.shard_map(
        shards,
        mesh=mesh,
        in_specs=(
            P(None, "dp", "tensor"),
            P(None, "dp"),
            P(),
            P(),
            P(),
            P(None, "tensor"),
            P("tensor", None),
            P(),
            P("dp", None, None),
        ),
        out_specs=(P("dp", None, "tensor"), P(None, "dp", "tensor")),
        check_vma=False,
    )
```

```python
import jax
import jax.numpy as jnp
from jax import lax
from jax.experimental import pallas as pl
from jax.experimental.pallas import tpu as pltpu
from jax.sharding import PartitionSpec as P

F = 256
D = 192
K = 8
NF = 8
S = 4
DW = 32
TP = 6
DP = 128
TURN = 79
DP_ORDER = [(q + TURN) % DP for q in range(DP)]
PEERS = [4, 0, 2, 5, 1, 3]
H = 1024
FK = F * K
ROW = DW * S
LARGE = 53_000_000
WHOLE = 66_600_000
CUT = 1024
bf16 = jnp.bfloat16
f32 = jnp.float32

VMEM = pl.BlockSpec(memory_space=pltpu.VMEM)
SMEM = pl.BlockSpec(memory_space=pltpu.SMEM)
HBM = pl.BlockSpec(memory_space=pltpu.HBM)


def iota(shape, dim):
    return lax.broadcasted_iota(jnp.int32, shape, dim)


def dot(a, b):
    return jnp.dot(a, b, preferred_element_type=f32)


def dot_nt(a, b):
    return lax.dot_general(a, b, (((1,), (1,)), ((), ())), preferred_element_type=f32)


def split(x):
    hi = x.astype(bf16)
    return hi, (x - hi.astype(f32)).astype(bf16)


def rows(parts):
    return jnp.concatenate(parts, axis=0)


def lanes(parts):
    return jnp.concatenate(parts, axis=1)


def own_sample():
    shape = (S * K, ROW)
    return iota(shape, 0) // K == iota(shape, 1) // DW


def expander():
    shape = (32, 256)
    return jnp.where(iota(shape, 0) == iota(shape, 1) // K, 1.0, 0.0).astype(bf16)


def own_rank():
    shape = (256, 256)
    return iota(shape, 0) % K == iota(shape, 1) % K


def pool_kernel(sums_hbm, len_hbm, out_ref, sums_ref, len_ref, scr, pairs, sem):
    sums_copy = pltpu.make_async_copy(sums_hbm, sums_ref, sem.at[0])
    len_copy = pltpu.make_async_copy(len_hbm, len_ref, sem.at[1])
    sums_copy.start()
    len_copy.start()
    len_copy.wait()
    length = len_ref[...].astype(f32)
    sums_copy.wait()
    for j in range(2):
        scr[j] = (sums_ref[j].astype(f32) / length[j : j + 1]).T
        pairs[pl.ds(j, DP, stride=2), :] = lanes(
            [scr[j, pl.ds(s, DP, stride=S), :] for s in range(S)]
        )
    turned = rows([pairs[2 * TURN :, :], pairs[: 2 * TURN, :]]) if TURN else pairs[...]
    out_ref[...] = turned.astype(bf16)


def slot_kernel(slot_ref, fm_ref, lc_ref, hot_ref, vt_ref):
    onehot = jnp.where(slot_ref[...] == (iota((F, F), 0) + 2 * TURN) % F, 1.0, 0.0).astype(bf16)
    hot_ref[...] = onehot
    both = rows([fm_ref[...].astype(f32), lc_ref[...].astype(f32)]).astype(bf16)
    vt_ref[...] = dot_nt(both, onehot).astype(bf16)


def gram_kernel(x_ref, vt_ref, hot_ref, g_ref, x_out, cb_ref, lin_ref):
    x = x_ref[...]
    x_out[...] = x
    y = dot(vt_ref[...], x)
    for s in range(S):
        lin_ref[s] = y[K:, s * DW : (s + 1) * DW].astype(bf16)
    hi, lo = split(jnp.where(own_sample(), rows([y[:K]] * S), 0.0))
    cb = rows([hi, lo])
    cb_ref[...] = cb
    g = dot_nt(cb, x)
    g = (g[:32] + g[32:]).reshape(S, K, F)
    mean = jnp.sum(jnp.sum(g, axis=2, keepdims=True), axis=1, keepdims=True) / FK
    g = (g - mean).reshape(S * K, F).astype(bf16)
    g = dot(g, hot_ref[...]).astype(bf16)
    for t in range(TP):
        g_ref[t] = g


def prep_kernel(
    rank_ref, cot_ref, vt_ref, after_ref, up_hbm, ow_hbm, dh_ref, cotl_ref, v_ref, up_out, ow_ref, cot_scr, sem
):
    ow_copy = pltpu.make_async_copy(ow_hbm, ow_ref, sem.at[0])
    up_copy = pltpu.make_async_copy(up_hbm.at[pl.ds(0, CUT)], up_out, sem.at[1])
    ow_copy.start()
    up_copy.start()
    cot_scr[...] = cot_ref[...].astype(f32)
    vt = vt_ref[...].astype(f32)
    v = vt.T
    v_ref[...] = lanes([v[:, :K], v]).astype(bf16)
    rank = rank_ref[0]
    parts = []
    for s in range(S):
        block = cot_scr[s, NF:, :]
        own = jnp.zeros((K, DW), f32)
        for t in range(TP):
            own = jnp.where(rank == t, block[:, t * DW : (t + 1) * DW], own)
        parts.append(own)
    cotl_ref[...] = lanes(parts)
    cot_fm = lanes([cot_scr[:, n, :] for n in range(NF)]).astype(bf16)
    ow_copy.wait()
    dh_ref[...] = dot_nt(cot_fm, ow_ref[...])
    up_copy.wait()


def mlp_kernel(g_ref, gain_ref, dh_ref, lo_ref, up_hbm, ow_hbm, c_ref, wh_ref, sc_ref, hi_ref, ow_ref, sem):
    up_copy = pltpu.make_async_copy(up_hbm.at[pl.ds(CUT, FK - CUT)], hi_ref, sem.at[0])
    ow_copy = pltpu.make_async_copy(ow_hbm, ow_ref, sem.at[1])
    up_copy.start()
    ow_copy.start()
    g = g_ref[0].astype(f32)
    for t in range(1, TP):
        g = g + g_ref[t].astype(f32)
    g = rows([g[:, c * 32 : (c + 1) * 32] for c in range(8)])
    hi, lo = split(g)
    m = dot(rows([hi, lo]), expander())
    m = jnp.where(own_rank(), m[:256] + m[256:], 0.0)
    m = jnp.sum(m.reshape(8 * S, K, 256), axis=1)
    flat = lanes([m[c * S : (c + 1) * S] for c in range(8)])
    centered = flat - jnp.mean(flat, axis=1, keepdims=True)
    scale = lax.rsqrt(jnp.mean(centered * centered, axis=1, keepdims=True) + 1e-05)
    whitened = centered * scale
    wh_ref[...] = whitened
    sc_ref[...] = jnp.broadcast_to(scale, sc_ref.shape)
    normed = (whitened * gain_ref[...]).astype(bf16)
    up = dot(normed[:, :CUT], lo_ref[...])
    up_copy.wait()
    up = up + dot(normed[:, CUT:], hi_ref[...])
    sig = jax.nn.sigmoid(up)
    hidden = (up * sig).astype(bf16)
    d_up = (dh_ref[...] * (sig + up * sig * (1.0 - sig))).astype(bf16)
    d_lo = dot_nt(d_up, lo_ref[...]).astype(bf16)
    d_hi = dot_nt(d_up, hi_ref[...]).astype(bf16)
    ow_copy.wait()
    fm = dot(hidden, ow_ref[...])
    for q in range(TP):
        t = PEERS[q]
        c_ref[q, :, :CUT] = d_lo
        c_ref[q, :, CUT:FK] = d_hi
        c_ref[q, :, FK:] = lanes(
            [fm[:, n * D + t * DW : n * D + (t + 1) * DW] for n in range(NF)]
        ).astype(bf16)


def grad_kernel(c_ref, gain_ref, wh_ref, sc_ref, x_ref, cb_ref, v_ref, cotl_ref, hot_ref, z_ref, fm_ref):
    c = c_ref[0].astype(f32)
    for t in range(1, TP):
        c = c + c_ref[t].astype(f32)
    fm_ref[...] = c[:, FK:]
    wh = wh_ref[...]
    gb = c[:, :FK] * gain_ref[...]
    flat = sc_ref[:, :1] * (
        gb
        - jnp.mean(gb, axis=1, keepdims=True)
        - wh * jnp.mean(gb * wh, axis=1, keepdims=True)
    )
    spread = rows(
        [
            jnp.broadcast_to(flat[:, None, c * 256 : (c + 1) * 256], (S, K, 256)).reshape(S * K, 256)
            for c in range(8)
        ]
    )
    hi, lo = split(jnp.where(own_rank(), spread, 0.0))
    dg = dot_nt(rows([hi, lo]), expander())
    dg = dg[:256] + dg[256:]
    dg = lanes([dg[c * 32 : (c + 1) * 32] for c in range(8)])
    hi, lo = split(dg)
    dg = dot_nt(rows([hi, lo]), hot_ref[...])
    dc = dot(dg.astype(bf16), x_ref[...])
    dc = jnp.where(own_sample(), dc[:32] + dc[32:], 0.0)
    dc = jnp.sum(dc.reshape(S, K, ROW), axis=0)
    dc_hi = dc.astype(bf16).astype(f32)
    cb = cb_ref[...].astype(f32)
    right = rows([cb[:32], cb[:32], cb[32:], dc_hi, dc - dc_hi, cotl_ref[...]]).astype(bf16)
    dgt = dg.T.astype(bf16)
    left = lanes([dgt, dgt[:, :32], v_ref[...]])
    z_ref[...] = dot(left, right).astype(bf16)


def unpool_kernel(z_ref, len_ref, fm_ref, lin_ref, out_ref, layer_ref, pairs, scr, layer):
    for n in range(NF):
        layer[:, n, :] = fm_ref[:, n * DW : (n + 1) * DW]
    layer[:, NF:, :] = lin_ref[...].astype(f32)
    layer_ref[...] = layer[...].astype(bf16)
    z = z_ref[...].astype(f32)
    pairs[...] = rows([z[F - 2 * TURN :], z[: F - 2 * TURN]]) if TURN else z
    for j in range(2):
        z = pairs[pl.ds(j, DP, stride=2), :]
        for s in range(S):
            scr[j, pl.ds(s, DP, stride=S), :] = z[:, s * DW : (s + 1) * DW]
        out_ref[j] = (scr[j].T / len_ref[j : j + 1, :].astype(f32)).astype(bf16)


def call(name, kernel, outs, args, specs=None, scratch=(), flops=0, nbytes=0, limit=16 * 2**20):
    many = len(outs) > 1
    shapes = [jax.ShapeDtypeStruct(s, d) for s, d in outs]
    return pl.pallas_call(
        kernel,
        out_shape=shapes if many else shapes[0],
        in_specs=specs or [VMEM] * len(args),
        out_specs=[VMEM] * len(outs) if many else VMEM,
        scratch_shapes=list(scratch),
        compiler_params=pltpu.CompilerParams(vmem_limit_bytes=limit),
        name=name,
        cost_estimate=pl.CostEstimate(flops=flops, bytes_accessed=nbytes, transcendentals=0)
        if flops
        else None,
    )(*args)


def exchange(x, axis, order):
    return lax.all_to_all(x, axis, split_axis=0, concat_axis=0, axis_index_groups=[order], tiled=True)


def shards(
    table_sums,
    bag_lengths,
    feature_slot,
    fm_project,
    ln_gain,
    up_weight,
    out_weight,
    lc_weight,
    cotangent,
):
    samples = table_sums.shape[0]
    sums_t = jnp.transpose(table_sums, (1, 2, 0))
    len_t = jnp.transpose(bag_lengths, (1, 0))
    dma = pltpu.SemaphoreType.DMA
    pooled = call(
        "pool",
        pool_kernel,
        [((F, ROW), bf16)],
        (sums_t, len_t),
        [HBM, HBM],
        [
            pltpu.VMEM((2, DW, samples), bf16),
            pltpu.VMEM((2, samples), jnp.int32),
            pltpu.VMEM((2, samples, DW), f32),
            pltpu.VMEM((F, ROW), f32),
            dma((2,)),
        ],
        limit=WHOLE,
    )
    arrived = exchange(pooled.reshape(DP, 2, ROW), "dp", DP_ORDER).reshape(F, ROW)
    hot, vt = call(
        "slots",
        slot_kernel,
        [((F, F), bf16), ((2 * K, F), bf16)],
        (feature_slot.reshape(1, F), fm_project.T, lc_weight.T),
    )
    g6, x, cb, lin = call(
        "gram",
        gram_kernel,
        [((TP, S * K, F), bf16), ((F, ROW), bf16), ((2 * S * K, ROW), bf16), ((S, K, DW), bf16)],
        (arrived, vt, hot),
    )
    g6 = exchange(g6, "tensor", PEERS)
    rank = lax.axis_index("tensor").astype(jnp.int32).reshape(1)
    dh, cotl, v, up_lo = call(
        "prep",
        prep_kernel,
        [((S, H), f32), ((K, ROW), f32), ((F, 3 * K), bf16), ((CUT, H), bf16)],
        (rank, cotangent, vt, cb, up_weight, out_weight),
        [SMEM, VMEM, VMEM, VMEM, HBM, HBM],
        [pltpu.VMEM((H, NF * D), bf16), pltpu.VMEM((S, 2 * NF, D), f32), dma((2,))],
        flops=2 * S * H * NF * D,
        nbytes=2 * (H * NF * D + CUT * H),
        limit=LARGE,
    )
    gain = ln_gain.reshape(1, FK)
    c6, wh, sc = call(
        "mlp",
        mlp_kernel,
        [((TP, S, FK + NF * DW), bf16), ((S, FK), f32), ((S, 128), f32)],
        (g6, gain, dh, up_lo, up_weight, out_weight),
        [VMEM, VMEM, VMEM, VMEM, HBM, HBM],
        [pltpu.VMEM((FK - CUT, H), bf16), pltpu.VMEM((H, NF * D), bf16), dma((2,))],
        limit=LARGE,
    )
    c6 = exchange(c6, "tensor", PEERS)
    z, fm = call(
        "grad",
        grad_kernel,
        [((F, ROW), bf16), ((S, NF * DW), f32)],
        (c6, gain, wh, sc, x, cb, v, cotl, hot),
    )
    back = exchange(z.reshape(DP, 2, ROW), "dp", DP_ORDER).reshape(F, ROW)
    grad_t, layer_out = call(
        "unpool",
        unpool_kernel,
        [((2, DW, samples), bf16), ((S, 2 * NF, DW), bf16)],
        (back, len_t, fm, lin),
        None,
        [pltpu.VMEM((F, ROW), f32), pltpu.VMEM((2, samples, DW), f32), pltpu.VMEM((S, 2 * NF, DW), f32)],
    )
    return (layer_out, jnp.transpose(grad_t, (2, 0, 1)))


def solution(mesh):
    return jax.shard_map(
        shards,
        mesh=mesh,
        in_specs=(
            P(None, "dp", "tensor"),
            P(None, "dp"),
            P(),
            P(),
            P(),
            P(None, "tensor"),
            P("tensor", None),
            P(),
            P("dp", None, None),
        ),
        out_specs=(P("dp", None, "tensor"), P(None, "dp", "tensor")),
        check_vma=False,
    )
```

```python
import jax
import jax.numpy as jnp
from jax import lax
from jax.experimental import pallas as pl
from jax.experimental.pallas import tpu as pltpu
from jax.sharding import PartitionSpec as P

F = 256
D = 192
K = 8
NF = 8
S = 4
DW = 32
TP = 6
DP = 128
TURN = 79
DP_ORDER = [(q + TURN) % DP for q in range(DP)]
PEERS = [4, 0, 1, 2, 3, 5]
H = 1024
FK = F * K
ROW = DW * S
LARGE = 53_000_000
WHOLE = 66_600_000
CUT = 1024
bf16 = jnp.bfloat16
f32 = jnp.float32

VMEM = pl.BlockSpec(memory_space=pltpu.VMEM)
SMEM = pl.BlockSpec(memory_space=pltpu.SMEM)
HBM = pl.BlockSpec(memory_space=pltpu.HBM)


def iota(shape, dim):
    return lax.broadcasted_iota(jnp.int32, shape, dim)


def dot(a, b):
    return jnp.dot(a, b, preferred_element_type=f32)


def dot_nt(a, b):
    return lax.dot_general(a, b, (((1,), (1,)), ((), ())), preferred_element_type=f32)


def split(x):
    hi = x.astype(bf16)
    return hi, (x - hi.astype(f32)).astype(bf16)


def rows(parts):
    return jnp.concatenate(parts, axis=0)


def lanes(parts):
    return jnp.concatenate(parts, axis=1)


def own_sample():
    shape = (S * K, ROW)
    return iota(shape, 0) // K == iota(shape, 1) // DW


def expander():
    shape = (32, 256)
    return jnp.where(iota(shape, 0) == iota(shape, 1) // K, 1.0, 0.0).astype(bf16)


def own_rank():
    shape = (256, 256)
    return iota(shape, 0) % K == iota(shape, 1) % K


def pool_kernel(sums_hbm, len_hbm, out_ref, sums_ref, len_ref, scr, pairs, sem):
    sums_copy = pltpu.make_async_copy(sums_hbm, sums_ref, sem.at[0])
    len_copy = pltpu.make_async_copy(len_hbm, len_ref, sem.at[1])
    sums_copy.start()
    len_copy.start()
    len_copy.wait()
    length = len_ref[...].astype(f32)
    sums_copy.wait()
    for j in range(2):
        scr[j] = (sums_ref[j].astype(f32) / length[j : j + 1]).T
        pairs[pl.ds(j, DP, stride=2), :] = lanes(
            [scr[j, pl.ds(s, DP, stride=S), :] for s in range(S)]
        )
    turned = rows([pairs[2 * TURN :, :], pairs[: 2 * TURN, :]]) if TURN else pairs[...]
    out_ref[...] = turned.astype(bf16)


def slot_kernel(slot_ref, fm_ref, lc_ref, hot_ref, vt_ref):
    onehot = jnp.where(slot_ref[...] == (iota((F, F), 0) + 2 * TURN) % F, 1.0, 0.0).astype(bf16)
    hot_ref[...] = onehot
    both = rows([fm_ref[...].astype(f32), lc_ref[...].astype(f32)]).astype(bf16)
    vt_ref[...] = dot_nt(both, onehot).astype(bf16)


def gram_kernel(x_ref, vt_ref, hot_ref, g_ref, x_out, cb_ref, lin_ref):
    x = x_ref[...]
    x_out[...] = x
    y = dot(vt_ref[...], x)
    for s in range(S):
        lin_ref[s] = y[K:, s * DW : (s + 1) * DW].astype(bf16)
    hi, lo = split(jnp.where(own_sample(), rows([y[:K]] * S), 0.0))
    cb = rows([hi, lo])
    cb_ref[...] = cb
    g = dot_nt(cb, x)
    g = (g[:32] + g[32:]).reshape(S, K, F)
    mean = jnp.sum(jnp.sum(g, axis=2, keepdims=True), axis=1, keepdims=True) / FK
    g = (g - mean).reshape(S * K, F).astype(bf16)
    g = dot(g, hot_ref[...]).astype(bf16)
    for t in range(TP):
        g_ref[t] = g


def prep_kernel(
    rank_ref, cot_ref, vt_ref, after_ref, up_hbm, ow_hbm, dh_ref, cotl_ref, v_ref, up_out, ow_ref, cot_scr, sem
):
    ow_copy = pltpu.make_async_copy(ow_hbm, ow_ref, sem.at[0])
    up_copy = pltpu.make_async_copy(up_hbm.at[pl.ds(0, CUT)], up_out, sem.at[1])
    ow_copy.start()
    up_copy.start()
    cot_scr[...] = cot_ref[...].astype(f32)
    vt = vt_ref[...].astype(f32)
    v = vt.T
    v_ref[...] = lanes([v[:, :K], v]).astype(bf16)
    rank = rank_ref[0]
    parts = []
    for s in range(S):
        block = cot_scr[s, NF:, :]
        own = jnp.zeros((K, DW), f32)
        for t in range(TP):
            own = jnp.where(rank == t, block[:, t * DW : (t + 1) * DW], own)
        parts.append(own)
    cotl_ref[...] = lanes(parts)
    cot_fm = lanes([cot_scr[:, n, :] for n in range(NF)]).astype(bf16)
    ow_copy.wait()
    dh_ref[...] = dot_nt(cot_fm, ow_ref[...])
    up_copy.wait()


def mlp_kernel(g_ref, gain_ref, dh_ref, lo_ref, up_hbm, ow_hbm, c_ref, wh_ref, sc_ref, hi_ref, ow_ref, sem):
    up_copy = pltpu.make_async_copy(up_hbm.at[pl.ds(CUT, FK - CUT)], hi_ref, sem.at[0])
    ow_copy = pltpu.make_async_copy(ow_hbm, ow_ref, sem.at[1])
    up_copy.start()
    ow_copy.start()
    g = g_ref[0].astype(f32)
    for t in range(1, TP):
        g = g + g_ref[t].astype(f32)
    g = rows([g[:, c * 32 : (c + 1) * 32] for c in range(8)])
    hi, lo = split(g)
    m = dot(rows([hi, lo]), expander())
    m = jnp.where(own_rank(), m[:256] + m[256:], 0.0)
    m = jnp.sum(m.reshape(8 * S, K, 256), axis=1)
    flat = lanes([m[c * S : (c + 1) * S] for c in range(8)])
    centered = flat - jnp.mean(flat, axis=1, keepdims=True)
    scale = lax.rsqrt(jnp.mean(centered * centered, axis=1, keepdims=True) + 1e-05)
    whitened = centered * scale
    wh_ref[...] = whitened
    sc_ref[...] = jnp.broadcast_to(scale, sc_ref.shape)
    normed = (whitened * gain_ref[...]).astype(bf16)
    up = dot(normed[:, :CUT], lo_ref[...])
    up_copy.wait()
    up = up + dot(normed[:, CUT:], hi_ref[...])
    sig = jax.nn.sigmoid(up)
    hidden = (up * sig).astype(bf16)
    d_up = (dh_ref[...] * (sig + up * sig * (1.0 - sig))).astype(bf16)
    d_lo = dot_nt(d_up, lo_ref[...]).astype(bf16)
    d_hi = dot_nt(d_up, hi_ref[...]).astype(bf16)
    ow_copy.wait()
    fm = dot(hidden, ow_ref[...])
    for q in range(TP):
        t = PEERS[q]
        c_ref[q, :, :CUT] = d_lo
        c_ref[q, :, CUT:FK] = d_hi
        c_ref[q, :, FK:] = lanes(
            [fm[:, n * D + t * DW : n * D + (t + 1) * DW] for n in range(NF)]
        ).astype(bf16)


def grad_kernel(c_ref, gain_ref, wh_ref, sc_ref, x_ref, cb_ref, v_ref, cotl_ref, hot_ref, z_ref, fm_ref):
    c = c_ref[0].astype(f32)
    for t in range(1, TP):
        c = c + c_ref[t].astype(f32)
    fm_ref[...] = c[:, FK:]
    wh = wh_ref[...]
    gb = c[:, :FK] * gain_ref[...]
    flat = sc_ref[:, :1] * (
        gb
        - jnp.mean(gb, axis=1, keepdims=True)
        - wh * jnp.mean(gb * wh, axis=1, keepdims=True)
    )
    spread = rows(
        [
            jnp.broadcast_to(flat[:, None, c * 256 : (c + 1) * 256], (S, K, 256)).reshape(S * K, 256)
            for c in range(8)
        ]
    )
    hi, lo = split(jnp.where(own_rank(), spread, 0.0))
    dg = dot_nt(rows([hi, lo]), expander())
    dg = dg[:256] + dg[256:]
    dg = lanes([dg[c * 32 : (c + 1) * 32] for c in range(8)])
    hi, lo = split(dg)
    dg = dot_nt(rows([hi, lo]), hot_ref[...])
    dc = dot(dg.astype(bf16), x_ref[...])
    dc = jnp.where(own_sample(), dc[:32] + dc[32:], 0.0)
    dc = jnp.sum(dc.reshape(S, K, ROW), axis=0)
    dc_hi = dc.astype(bf16).astype(f32)
    cb = cb_ref[...].astype(f32)
    right = rows([cb[:32], cb[:32], cb[32:], dc_hi, dc - dc_hi, cotl_ref[...]]).astype(bf16)
    dgt = dg.T.astype(bf16)
    left = lanes([dgt, dgt[:, :32], v_ref[...]])
    z_ref[...] = dot(left, right).astype(bf16)


def unpool_kernel(z_ref, len_ref, fm_ref, lin_ref, out_ref, layer_ref, pairs, scr, layer):
    for n in range(NF):
        layer[:, n, :] = fm_ref[:, n * DW : (n + 1) * DW]
    layer[:, NF:, :] = lin_ref[...].astype(f32)
    layer_ref[...] = layer[...].astype(bf16)
    z = z_ref[...].astype(f32)
    pairs[...] = rows([z[F - 2 * TURN :], z[: F - 2 * TURN]]) if TURN else z
    for j in range(2):
        z = pairs[pl.ds(j, DP, stride=2), :]
        for s in range(S):
            scr[j, pl.ds(s, DP, stride=S), :] = z[:, s * DW : (s + 1) * DW]
        out_ref[j] = (scr[j].T / len_ref[j : j + 1, :].astype(f32)).astype(bf16)


def call(name, kernel, outs, args, specs=None, scratch=(), flops=0, nbytes=0, limit=16 * 2**20):
    many = len(outs) > 1
    shapes = [jax.ShapeDtypeStruct(s, d) for s, d in outs]
    return pl.pallas_call(
        kernel,
        out_shape=shapes if many else shapes[0],
        in_specs=specs or [VMEM] * len(args),
        out_specs=[VMEM] * len(outs) if many else VMEM,
        scratch_shapes=list(scratch),
        compiler_params=pltpu.CompilerParams(vmem_limit_bytes=limit),
        name=name,
        cost_estimate=pl.CostEstimate(flops=flops, bytes_accessed=nbytes, transcendentals=0)
        if flops
        else None,
    )(*args)


def exchange(x, axis, order):
    return lax.all_to_all(x, axis, split_axis=0, concat_axis=0, axis_index_groups=[order], tiled=True)


def shards(
    table_sums,
    bag_lengths,
    feature_slot,
    fm_project,
    ln_gain,
    up_weight,
    out_weight,
    lc_weight,
    cotangent,
):
    samples = table_sums.shape[0]
    sums_t = jnp.transpose(table_sums, (1, 2, 0))
    len_t = jnp.transpose(bag_lengths, (1, 0))
    dma = pltpu.SemaphoreType.DMA
    pooled = call(
        "pool",
        pool_kernel,
        [((F, ROW), bf16)],
        (sums_t, len_t),
        [HBM, HBM],
        [
            pltpu.VMEM((2, DW, samples), bf16),
            pltpu.VMEM((2, samples), jnp.int32),
            pltpu.VMEM((2, samples, DW), f32),
            pltpu.VMEM((F, ROW), f32),
            dma((2,)),
        ],
        limit=WHOLE,
    )
    arrived = exchange(pooled.reshape(DP, 2, ROW), "dp", DP_ORDER).reshape(F, ROW)
    hot, vt = call(
        "slots",
        slot_kernel,
        [((F, F), bf16), ((2 * K, F), bf16)],
        (feature_slot.reshape(1, F), fm_project.T, lc_weight.T),
    )
    g6, x, cb, lin = call(
        "gram",
        gram_kernel,
        [((TP, S * K, F), bf16), ((F, ROW), bf16), ((2 * S * K, ROW), bf16), ((S, K, DW), bf16)],
        (arrived, vt, hot),
    )
    g6 = exchange(g6, "tensor", PEERS)
    rank = lax.axis_index("tensor").astype(jnp.int32).reshape(1)
    dh, cotl, v, up_lo = call(
        "prep",
        prep_kernel,
        [((S, H), f32), ((K, ROW), f32), ((F, 3 * K), bf16), ((CUT, H), bf16)],
        (rank, cotangent, vt, cb, up_weight, out_weight),
        [SMEM, VMEM, VMEM, VMEM, HBM, HBM],
        [pltpu.VMEM((H, NF * D), bf16), pltpu.VMEM((S, 2 * NF, D), f32), dma((2,))],
        flops=2 * S * H * NF * D,
        nbytes=2 * (H * NF * D + CUT * H),
        limit=LARGE,
    )
    gain = ln_gain.reshape(1, FK)
    c6, wh, sc = call(
        "mlp",
        mlp_kernel,
        [((TP, S, FK + NF * DW), bf16), ((S, FK), f32), ((S, 128), f32)],
        (g6, gain, dh, up_lo, up_weight, out_weight),
        [VMEM, VMEM, VMEM, VMEM, HBM, HBM],
        [pltpu.VMEM((FK - CUT, H), bf16), pltpu.VMEM((H, NF * D), bf16), dma((2,))],
        limit=LARGE,
    )
    c6 = exchange(c6, "tensor", PEERS)
    z, fm = call(
        "grad",
        grad_kernel,
        [((F, ROW), bf16), ((S, NF * DW), f32)],
        (c6, gain, wh, sc, x, cb, v, cotl, hot),
    )
    back = exchange(z.reshape(DP, 2, ROW), "dp", DP_ORDER).reshape(F, ROW)
    grad_t, layer_out = call(
        "unpool",
        unpool_kernel,
        [((2, DW, samples), bf16), ((S, 2 * NF, DW), bf16)],
        (back, len_t, fm, lin),
        None,
        [pltpu.VMEM((F, ROW), f32), pltpu.VMEM((2, samples, DW), f32), pltpu.VMEM((S, 2 * NF, DW), f32)],
    )
    return (layer_out, jnp.transpose(grad_t, (2, 0, 1)))


def solution(mesh):
    return jax.shard_map(
        shards,
        mesh=mesh,
        in_specs=(
            P(None, "dp", "tensor"),
            P(None, "dp"),
            P(),
            P(),
            P(),
            P(None, "tensor"),
            P("tensor", None),
            P(),
            P("dp", None, None),
        ),
        out_specs=(P("dp", None, "tensor"), P(None, "dp", "tensor")),
        check_vma=False,
    )
```

```python
import jax
import jax.numpy as jnp
from jax import lax
from jax.experimental import pallas as pl
from jax.experimental.pallas import tpu as pltpu
from jax.sharding import PartitionSpec as P

F = 256
D = 192
K = 8
NF = 8
S = 4
DW = 32
TP = 6
DP = 128
TURN = 79
DP_ORDER = [(q + TURN) % DP for q in range(DP)]
PEERS_GRAD = [5, 0, 1, 2, 3, 4]
PEERS = [4, 0, 1, 2, 3, 5]
H = 1024
FK = F * K
ROW = DW * S
LARGE = 53_000_000
WHOLE = 66_600_000
CUT = 1024
bf16 = jnp.bfloat16
f32 = jnp.float32

VMEM = pl.BlockSpec(memory_space=pltpu.VMEM)
SMEM = pl.BlockSpec(memory_space=pltpu.SMEM)
HBM = pl.BlockSpec(memory_space=pltpu.HBM)


def iota(shape, dim):
    return lax.broadcasted_iota(jnp.int32, shape, dim)


def dot(a, b):
    return jnp.dot(a, b, preferred_element_type=f32)


def dot_nt(a, b):
    return lax.dot_general(a, b, (((1,), (1,)), ((), ())), preferred_element_type=f32)


def split(x):
    hi = x.astype(bf16)
    return hi, (x - hi.astype(f32)).astype(bf16)


def rows(parts):
    return jnp.concatenate(parts, axis=0)


def lanes(parts):
    return jnp.concatenate(parts, axis=1)


def own_sample():
    shape = (S * K, ROW)
    return iota(shape, 0) // K == iota(shape, 1) // DW


def expander():
    shape = (32, 256)
    return jnp.where(iota(shape, 0) == iota(shape, 1) // K, 1.0, 0.0).astype(bf16)


def own_rank():
    shape = (256, 256)
    return iota(shape, 0) % K == iota(shape, 1) % K


def pool_kernel(sums_hbm, len_hbm, out_ref, sums_ref, len_ref, scr, pairs, sem):
    sums_copy = pltpu.make_async_copy(sums_hbm, sums_ref, sem.at[0])
    len_copy = pltpu.make_async_copy(len_hbm, len_ref, sem.at[1])
    sums_copy.start()
    len_copy.start()
    len_copy.wait()
    length = len_ref[...].astype(f32)
    sums_copy.wait()
    for j in range(2):
        scr[j] = (sums_ref[j].astype(f32) / length[j : j + 1]).T
        pairs[pl.ds(j, DP, stride=2), :] = lanes(
            [scr[j, pl.ds(s, DP, stride=S), :] for s in range(S)]
        )
    turned = rows([pairs[2 * TURN :, :], pairs[: 2 * TURN, :]]) if TURN else pairs[...]
    out_ref[...] = turned.astype(bf16)


def slot_kernel(slot_ref, fm_ref, lc_ref, hot_ref, vt_ref):
    onehot = jnp.where(slot_ref[...] == (iota((F, F), 0) + 2 * TURN) % F, 1.0, 0.0).astype(bf16)
    hot_ref[...] = onehot
    both = rows([fm_ref[...].astype(f32), lc_ref[...].astype(f32)]).astype(bf16)
    vt_ref[...] = dot_nt(both, onehot).astype(bf16)


def gram_kernel(x_ref, vt_ref, hot_ref, g_ref, x_out, cb_ref, lin_ref):
    x = x_ref[...]
    x_out[...] = x
    y = dot(vt_ref[...], x)
    for s in range(S):
        lin_ref[s] = y[K:, s * DW : (s + 1) * DW].astype(bf16)
    hi, lo = split(jnp.where(own_sample(), rows([y[:K]] * S), 0.0))
    cb = rows([hi, lo])
    cb_ref[...] = cb
    g = dot_nt(cb, x)
    g = (g[:32] + g[32:]).reshape(S, K, F)
    mean = jnp.sum(jnp.sum(g, axis=2, keepdims=True), axis=1, keepdims=True) / FK
    g = (g - mean).reshape(S * K, F).astype(bf16)
    g = dot(g, hot_ref[...]).astype(bf16)
    for t in range(TP):
        g_ref[t] = g


def prep_kernel(
    rank_ref, cot_ref, vt_ref, after_ref, up_hbm, ow_hbm, dh_ref, cotl_ref, v_ref, up_out, ow_ref, cot_scr, sem
):
    ow_copy = pltpu.make_async_copy(ow_hbm, ow_ref, sem.at[0])
    up_copy = pltpu.make_async_copy(up_hbm.at[pl.ds(0, CUT)], up_out, sem.at[1])
    ow_copy.start()
    up_copy.start()
    cot_scr[...] = cot_ref[...].astype(f32)
    vt = vt_ref[...].astype(f32)
    v = vt.T
    v_ref[...] = lanes([v[:, :K], v]).astype(bf16)
    rank = rank_ref[0]
    parts = []
    for s in range(S):
        block = cot_scr[s, NF:, :]
        own = jnp.zeros((K, DW), f32)
        for t in range(TP):
            own = jnp.where(rank == t, block[:, t * DW : (t + 1) * DW], own)
        parts.append(own)
    cotl_ref[...] = lanes(parts)
    cot_fm = lanes([cot_scr[:, n, :] for n in range(NF)]).astype(bf16)
    ow_copy.wait()
    dh_ref[...] = dot_nt(cot_fm, ow_ref[...])
    up_copy.wait()


def mlp_kernel(g_ref, gain_ref, dh_ref, lo_ref, up_hbm, ow_hbm, c_ref, wh_ref, sc_ref, hi_ref, ow_ref, sem):
    up_copy = pltpu.make_async_copy(up_hbm.at[pl.ds(CUT, FK - CUT)], hi_ref, sem.at[0])
    ow_copy = pltpu.make_async_copy(ow_hbm, ow_ref, sem.at[1])
    up_copy.start()
    ow_copy.start()
    g = g_ref[0].astype(f32)
    for t in range(1, TP):
        g = g + g_ref[t].astype(f32)
    g = rows([g[:, c * 32 : (c + 1) * 32] for c in range(8)])
    hi, lo = split(g)
    m = dot(rows([hi, lo]), expander())
    m = jnp.where(own_rank(), m[:256] + m[256:], 0.0)
    m = jnp.sum(m.reshape(8 * S, K, 256), axis=1)
    flat = lanes([m[c * S : (c + 1) * S] for c in range(8)])
    centered = flat - jnp.mean(flat, axis=1, keepdims=True)
    scale = lax.rsqrt(jnp.mean(centered * centered, axis=1, keepdims=True) + 1e-05)
    whitened = centered * scale
    wh_ref[...] = whitened
    sc_ref[...] = jnp.broadcast_to(scale, sc_ref.shape)
    normed = (whitened * gain_ref[...]).astype(bf16)
    up = dot(normed[:, :CUT], lo_ref[...])
    up_copy.wait()
    up = up + dot(normed[:, CUT:], hi_ref[...])
    sig = jax.nn.sigmoid(up)
    hidden = (up * sig).astype(bf16)
    d_up = (dh_ref[...] * (sig + up * sig * (1.0 - sig))).astype(bf16)
    d_lo = dot_nt(d_up, lo_ref[...]).astype(bf16)
    d_hi = dot_nt(d_up, hi_ref[...]).astype(bf16)
    ow_copy.wait()
    fm = dot(hidden, ow_ref[...])
    for q in range(TP):
        t = PEERS_GRAD[q]
        c_ref[q, :, :CUT] = d_lo
        c_ref[q, :, CUT:FK] = d_hi
        c_ref[q, :, FK:] = lanes(
            [fm[:, n * D + t * DW : n * D + (t + 1) * DW] for n in range(NF)]
        ).astype(bf16)


def grad_kernel(c_ref, gain_ref, wh_ref, sc_ref, x_ref, cb_ref, v_ref, cotl_ref, hot_ref, z_ref, fm_ref):
    c = c_ref[0].astype(f32)
    for t in range(1, TP):
        c = c + c_ref[t].astype(f32)
    fm_ref[...] = c[:, FK:]
    wh = wh_ref[...]
    gb = c[:, :FK] * gain_ref[...]
    flat = sc_ref[:, :1] * (
        gb
        - jnp.mean(gb, axis=1, keepdims=True)
        - wh * jnp.mean(gb * wh, axis=1, keepdims=True)
    )
    spread = rows(
        [
            jnp.broadcast_to(flat[:, None, c * 256 : (c + 1) * 256], (S, K, 256)).reshape(S * K, 256)
            for c in range(8)
        ]
    )
    hi, lo = split(jnp.where(own_rank(), spread, 0.0))
    dg = dot_nt(rows([hi, lo]), expander())
    dg = dg[:256] + dg[256:]
    dg = lanes([dg[c * 32 : (c + 1) * 32] for c in range(8)])
    hi, lo = split(dg)
    dg = dot_nt(rows([hi, lo]), hot_ref[...])
    dc = dot(dg.astype(bf16), x_ref[...])
    dc = jnp.where(own_sample(), dc[:32] + dc[32:], 0.0)
    dc = jnp.sum(dc.reshape(S, K, ROW), axis=0)
    dc_hi = dc.astype(bf16).astype(f32)
    cb = cb_ref[...].astype(f32)
    right = rows([cb[:32], cb[:32], cb[32:], dc_hi, dc - dc_hi, cotl_ref[...]]).astype(bf16)
    dgt = dg.T.astype(bf16)
    left = lanes([dgt, dgt[:, :32], v_ref[...]])
    z_ref[...] = dot(left, right).astype(bf16)


def unpool_kernel(z_ref, len_ref, fm_ref, lin_ref, out_ref, layer_ref, pairs, scr, layer):
    for n in range(NF):
        layer[:, n, :] = fm_ref[:, n * DW : (n + 1) * DW]
    layer[:, NF:, :] = lin_ref[...].astype(f32)
    layer_ref[...] = layer[...].astype(bf16)
    z = z_ref[...].astype(f32)
    pairs[...] = rows([z[F - 2 * TURN :], z[: F - 2 * TURN]]) if TURN else z
    for j in range(2):
        z = pairs[pl.ds(j, DP, stride=2), :]
        for s in range(S):
            scr[j, pl.ds(s, DP, stride=S), :] = z[:, s * DW : (s + 1) * DW]
        out_ref[j] = (scr[j].T / len_ref[j : j + 1, :].astype(f32)).astype(bf16)


def call(name, kernel, outs, args, specs=None, scratch=(), flops=0, nbytes=0, limit=16 * 2**20):
    many = len(outs) > 1
    shapes = [jax.ShapeDtypeStruct(s, d) for s, d in outs]
    return pl.pallas_call(
        kernel,
        out_shape=shapes if many else shapes[0],
        in_specs=specs or [VMEM] * len(args),
        out_specs=[VMEM] * len(outs) if many else VMEM,
        scratch_shapes=list(scratch),
        compiler_params=pltpu.CompilerParams(vmem_limit_bytes=limit),
        name=name,
        cost_estimate=pl.CostEstimate(flops=flops, bytes_accessed=nbytes, transcendentals=0)
        if flops
        else None,
    )(*args)


def exchange(x, axis, order):
    return lax.all_to_all(x, axis, split_axis=0, concat_axis=0, axis_index_groups=[order], tiled=True)


def shards(
    table_sums,
    bag_lengths,
    feature_slot,
    fm_project,
    ln_gain,
    up_weight,
    out_weight,
    lc_weight,
    cotangent,
):
    samples = table_sums.shape[0]
    sums_t = jnp.transpose(table_sums, (1, 2, 0))
    len_t = jnp.transpose(bag_lengths, (1, 0))
    dma = pltpu.SemaphoreType.DMA
    pooled = call(
        "pool",
        pool_kernel,
        [((F, ROW), bf16)],
        (sums_t, len_t),
        [HBM, HBM],
        [
            pltpu.VMEM((2, DW, samples), bf16),
            pltpu.VMEM((2, samples), jnp.int32),
            pltpu.VMEM((2, samples, DW), f32),
            pltpu.VMEM((F, ROW), f32),
            dma((2,)),
        ],
        limit=WHOLE,
    )
    arrived = exchange(pooled.reshape(DP, 2, ROW), "dp", DP_ORDER).reshape(F, ROW)
    hot, vt = call(
        "slots",
        slot_kernel,
        [((F, F), bf16), ((2 * K, F), bf16)],
        (feature_slot.reshape(1, F), fm_project.T, lc_weight.T),
    )
    g6, x, cb, lin = call(
        "gram",
        gram_kernel,
        [((TP, S * K, F), bf16), ((F, ROW), bf16), ((2 * S * K, ROW), bf16), ((S, K, DW), bf16)],
        (arrived, vt, hot),
    )
    g6 = exchange(g6, "tensor", PEERS)
    rank = lax.axis_index("tensor").astype(jnp.int32).reshape(1)
    dh, cotl, v, up_lo = call(
        "prep",
        prep_kernel,
        [((S, H), f32), ((K, ROW), f32), ((F, 3 * K), bf16), ((CUT, H), bf16)],
        (rank, cotangent, vt, cb, up_weight, out_weight),
        [SMEM, VMEM, VMEM, VMEM, HBM, HBM],
        [pltpu.VMEM((H, NF * D), bf16), pltpu.VMEM((S, 2 * NF, D), f32), dma((2,))],
        flops=2 * S * H * NF * D,
        nbytes=2 * (H * NF * D + CUT * H),
        limit=LARGE,
    )
    gain = ln_gain.reshape(1, FK)
    c6, wh, sc = call(
        "mlp",
        mlp_kernel,
        [((TP, S, FK + NF * DW), bf16), ((S, FK), f32), ((S, 128), f32)],
        (g6, gain, dh, up_lo, up_weight, out_weight),
        [VMEM, VMEM, VMEM, VMEM, HBM, HBM],
        [pltpu.VMEM((FK - CUT, H), bf16), pltpu.VMEM((H, NF * D), bf16), dma((2,))],
        limit=LARGE,
    )
    c6 = exchange(c6, "tensor", PEERS_GRAD)
    z, fm = call(
        "grad",
        grad_kernel,
        [((F, ROW), bf16), ((S, NF * DW), f32)],
        (c6, gain, wh, sc, x, cb, v, cotl, hot),
    )
    back = exchange(z.reshape(DP, 2, ROW), "dp", DP_ORDER).reshape(F, ROW)
    grad_t, layer_out = call(
        "unpool",
        unpool_kernel,
        [((2, DW, samples), bf16), ((S, 2 * NF, DW), bf16)],
        (back, len_t, fm, lin),
        None,
        [pltpu.VMEM((F, ROW), f32), pltpu.VMEM((2, samples, DW), f32), pltpu.VMEM((S, 2 * NF, DW), f32)],
    )
    return (layer_out, jnp.transpose(grad_t, (2, 0, 1)))


def solution(mesh):
    return jax.shard_map(
        shards,
        mesh=mesh,
        in_specs=(
            P(None, "dp", "tensor"),
            P(None, "dp"),
            P(),
            P(),
            P(),
            P(None, "tensor"),
            P("tensor", None),
            P(),
            P("dp", None, None),
        ),
        out_specs=(P("dp", None, "tensor"), P(None, "dp", "tensor")),
        check_vma=False,
    )
```
